256 devices in a mesh: lsec: 8 (over x, y_hi), rsec: 32 (over z, y_lo, core).
Axes of the slice: x: 4, y: 4 (y_hi: 2, y_lo: 2; y = y_hi * 2 + y_lo), z: 8, core: 2. Of those that a mesh axis runs over, the one named last changes fastest.
Arguments:
- psi: bfloat16 [32, 64, 256, 256], P('lsec', 'rsec'), may hold values from -6 to 6
- left_env: bfloat16 [32, 4, 256, 256], P('lsec'), may hold values from -0.375 to 0.375
- right_env: bfloat16 [64, 4, 256, 256], P('rsec'), may hold values from -0.1875 to 0.1875
- energies: float32 [32, 64], P('lsec', 'rsec'), may hold values from 0.5 to 3
- coef_num: int32 [2], replicated, may hold values from 3 to 9
- coef_den: int32 [2], replicated, may hold values from 4 to 8
Outputs:
- vector_out: bfloat16 [32, 64, 256, 256], P('lsec', 'rsec')
- ritz: float32 [3], replicated
The draws below stay inside these ranges and needn't reach their ends.
All inputs are finite; a program needn't handle non-finite values.
Results may differ from the reference program's by a relative error of at most 0.015.
Values may be sent and summed in bfloat16 or wider, within the bound.
No kernel may reach another device: no remote copies, remote signals or barrier semaphores. Data moves between devices by JAX's collectives and lax.ppermute only.
A program may use at most 64 MiB of HBM per device.

```python
import jax
import jax.numpy as jnp
from jax import lax

B = 256
DIAG = 2
HOPS = 1
ITERS = 3
TERMS = 4
NA = 32
NB = 64


def block_levels(rng, dims, shards, smallest, top_value):
    loudness, own = 1.0, jax.random.fold_in(rng, 6)
    for dim, parts in shards:
        draws = jnp.exp(jax.random.uniform(jax.random.fold_in(own, dim), (parts,), jnp.float32, smallest / len(shards), top_value / len(shards)))
        loudness = loudness * jnp.repeat(draws, dims[dim] // parts).reshape([-1 if axis == dim else 1 for axis in range(len(dims))])
    return loudness


def centred(own_key, shape, width, bound, shards=(), kind=jnp.bfloat16):
    entries = jax.random.normal(own_key, shape, jnp.float32) * width
    if len(shards) > 0:
        entries = block_levels(own_key, shape, shards, -0.22, 0.18) * entries
    return jnp.clip(entries, min=-bound, max=bound).astype(kind)


def setup_inputs(seed: int = 0) -> dict:
    arg_keys = jax.random.split(jax.random.key(seed), 7)
    psi = centred(arg_keys[0], (NA, NB, B, B), 1.0, 6.0, ((0, 8), (1, 32)))
    left_env = centred(arg_keys[1], (NA, TERMS, B, B), B ** -0.5, 0.375, ((0, 8),))
    right_env = centred(arg_keys[2], (NB, TERMS, B, B), (B * TERMS) ** -0.5, 0.1875, ((0, 32),))
    energies = jnp.clip(0.5 + 2.5 * jax.random.uniform(arg_keys[3], (NA, NB), jnp.float32) ** block_levels(arg_keys[3], (NA, NB), ((0, 8), (1, 32)), -0.2, 0.2), 0.5, 3.0)
    coef_num = jax.random.randint(arg_keys[4], (ITERS - 1,), 3, 10).astype(jnp.int32)
    coef_den = jax.random.randint(arg_keys[5], (ITERS - 1,), 4, 9).astype(jnp.int32)
    return {"psi": psi, "left_env": left_env, "right_env": right_env, "energies": energies, "coef_num": coef_num, "coef_den": coef_den}


eps = 1e-06

def matvec(vec, left_env, right_env, energies):
    vals = vec.astype(jnp.float32)
    padded = jnp.pad(vals, ((1, 1), (1, 1), (0, 0), (0, 0)))
    plus_blocks = padded[:-2, 2:]
    minus_blocks = padded[2:, :-2]
    total = energies[:, :, None, None] * vals
    left_all = left_env.astype(jnp.float32)
    right_all = right_env.astype(jnp.float32)
    for term in range(DIAG + 2 * HOPS):
        if term < DIAG:
            source = vals
        elif term < DIAG + HOPS:
            source = plus_blocks
        else:
            source = minus_blocks
        inner = jnp.einsum('aij,abjk->abik', left_all[:, term], source).astype(jnp.bfloat16)
        total = total + jnp.einsum('abik,blk->abil', inner.astype(jnp.float32), right_all[:, term])
    return total

def reference(psi, left_env, right_env, energies, coef_num, coef_den):
    count = 1.0 / float(psi.size)
    start_vals = psi.astype(jnp.float32)
    start = jnp.sum(start_vals * start_vals) * count
    vec = (start_vals * lax.rsqrt(start + eps)).astype(jnp.bfloat16)
    previous = jnp.zeros(psi.shape, jnp.float32)
    thetas = []
    for step in range(ITERS):
        sigma = matvec(vec, left_env, right_env, energies)
        vals = vec.astype(jnp.float32)
        theta = jnp.sum(vals * sigma) * count
        thetas.append(theta)
        if step == 0:
            coef = jnp.float32(0.0)
        else:
            coef = coef_num[step - 1].astype(jnp.float32) / coef_den[step - 1].astype(jnp.float32)
        resid = sigma - theta * vals - coef * previous
        norm_sq = jnp.sum(resid * resid) * count
        previous = vals
        vec = (resid * lax.rsqrt(norm_sq + eps)).astype(jnp.bfloat16)
    return (vec, jnp.stack(thetas))
```

```python
import jax
import jax.numpy as jnp
from jax import lax
from jax.sharding import PartitionSpec as P

DIAG = 2
HOPS = 1
ITERS = 3
AXES = ("lsec", "rsec")
eps = 1e-06
SHIFT = 1.75
SHRINK = 8.0


def shift_blocks(block, down, right):
    rows, cols = lax.axis_size("lsec"), lax.axis_size("rsec")
    pairs = [
        (row * cols + col, (row + down) * cols + col + right)
        for row in range(rows)
        for col in range(cols)
        if 0 <= row + down < rows and 0 <= col + right < cols
    ]
    return lax.ppermute(block, AXES, pairs)


def add_terms(left_env, right_env, source, first, number, total):
    for term in range(first, first + number):
        inner = jnp.einsum(
            "aij,abjk->abik", left_env[:, term], source, preferred_element_type=jnp.float32
        ).astype(jnp.bfloat16)
        total = total + jnp.einsum(
            "abik,blk->abil", inner, right_env[:, term], preferred_element_type=jnp.float32
        )
    return total


def matvec(vec, left_env, right_env, energies):
    total = energies[:, :, None, None] * vec.astype(jnp.float32)
    total = add_terms(left_env, right_env, vec, 0, DIAG, total)
    from_right = shift_blocks(vec[:-1, :1], 0, -1)
    from_left = shift_blocks(vec[1:, -1:], 0, 1)
    from_up = shift_blocks(vec[-1:, 1:], 1, 0)
    from_down = shift_blocks(vec[:1, :-1], -1, 0)
    up_right = shift_blocks(vec[-1:, :1], 1, -1)
    down_left = shift_blocks(vec[:1, -1:], -1, 1)
    plus_blocks = jnp.concatenate(
        [
            jnp.concatenate([from_up, up_right], axis=1),
            jnp.concatenate([vec[:-1, 1:], from_right], axis=1),
        ],
        axis=0,
    )
    minus_blocks = jnp.concatenate(
        [
            jnp.concatenate([from_left, vec[1:, :-1]], axis=1),
            jnp.concatenate([down_left, from_down], axis=1),
        ],
        axis=0,
    )
    total = add_terms(left_env, right_env, plus_blocks, DIAG, HOPS, total)
    total = add_terms(left_env, right_env, minus_blocks, DIAG + HOPS, HOPS, total)
    return total


def coefficient(coef_num, coef_den, step):
    if step == 0:
        return jnp.float32(0.0)
    return coef_num[step - 1].astype(jnp.float32) / coef_den[step - 1].astype(jnp.float32)


def stepwise(psi, left_env, right_env, energies, coef_num, coef_den, count):
    start_vals = psi.astype(jnp.float32)
    start = lax.psum(jnp.sum(start_vals * start_vals), AXES) * count
    vec = (start_vals * lax.rsqrt(start + eps)).astype(jnp.bfloat16)
    previous = jnp.zeros(psi.shape, jnp.float32)
    thetas = []
    for step in range(ITERS):
        sigma = matvec(vec, left_env, right_env, energies)
        vals = vec.astype(jnp.float32)
        coef = coefficient(coef_num, coef_den, step)
        theta = lax.psum(jnp.sum(vals * sigma), AXES) * count
        resid = sigma - theta * vals - coef * previous
        norm_sq = lax.psum(jnp.sum(resid * resid), AXES) * count
        thetas.append(theta)
        previous = vals
        vec = (resid * lax.rsqrt(norm_sq + eps)).astype(jnp.bfloat16)
    return (vec, jnp.stack(thetas))


def gather_sum(parts):
    devices = lax.axis_size("lsec") * lax.axis_size("rsec")
    row = jnp.zeros((1, 128), jnp.float32).at[0, : parts.shape[0]].set(parts)
    sent = jnp.broadcast_to(row[None], (devices, 1, 128))
    return jnp.sum(lax.all_to_all(sent, AXES, 0, 0), axis=(0, 1))


def recursion(gram, coef_num, coef_den):
    def quad(left, right):
        return sum(
            left[i] * right[j] * gram[min(i, j)][max(i, j)]
            for i in range(len(left))
            for j in range(len(right))
        )

    scale = lax.rsqrt(gram[0][0] + eps)
    vec, previous = [scale], []
    thetas, fine = [], jnp.bool_(True)
    for step in range(ITERS):
        moved = [jnp.float32(0.0)] + vec
        theta = quad(vec, [SHIFT * entry for entry in vec]) + quad(vec, moved)
        thetas.append(theta)
        coef = coefficient(coef_num, coef_den, step)
        resid = list(moved)
        for i, entry in enumerate(vec):
            resid[i] = resid[i] + (SHIFT - theta) * entry
        for i, entry in enumerate(previous):
            resid[i] = resid[i] - coef * entry
        norm_sq = quad(resid, resid)
        lead = resid[-1]
        fine = fine & (lead * lead * gram[step + 1][step + 1] <= SHRINK * (norm_sq + eps))
        norm = lax.rsqrt(jnp.maximum(norm_sq, 0.0) + eps)
        previous = vec
        vec = [entry * norm for entry in resid]
    return vec, thetas, fine


def per_device(psi, left_env, right_env, energies, coef_num, coef_den):
    count = 1.0 / float(psi.size * lax.axis_size("lsec") * lax.axis_size("rsec"))
    basis = [psi]
    parts = [jnp.sum(psi.astype(jnp.float32) ** 2)]
    for step in range(ITERS):
        image = matvec(basis[-1], left_env, right_env, energies - SHIFT)
        if step < ITERS - 1:
            image = image.astype(jnp.bfloat16)
        basis.append(image)
        vals = image.astype(jnp.float32)
        for other in basis:
            parts.append(jnp.sum(vals * other.astype(jnp.float32)))
    sums = gather_sum(jnp.stack(parts) * count)
    gram = [[None] * (ITERS + 1) for _ in range(ITERS + 1)]
    place = 0
    for right in range(ITERS + 1):
        for left in range(right + 1):
            gram[left][right] = sums[place]
            place += 1
    weights, thetas, fine = recursion(gram, coef_num, coef_den)

    def combine():
        total = weights[0] * psi.astype(jnp.float32)
        for weight, vec in zip(weights[1:], basis[1:]):
            total = total + weight * vec.astype(jnp.float32)
        return total.astype(jnp.bfloat16), jnp.stack(thetas)

    def again():
        return stepwise(psi, left_env, right_env, energies, coef_num, coef_den, count)

    return lax.cond(fine, combine, again)


def solution(mesh):
    in_specs = (
        P("lsec", "rsec", None, None),
        P("lsec", None, None, None),
        P("rsec", None, None, None),
        P("lsec", "rsec"),
        P(),
        P(),
    )
    out_specs = (P("lsec", "rsec", None, None), P())
    return jax.shard_map(
        per_device, mesh=mesh, in_specs=in_specs, out_specs=out_specs, check_vma=False
    )
```

```python
import jax
import jax.numpy as jnp
from jax import lax
from jax.experimental import pallas as pl
from jax.experimental.pallas import tpu as pltpu
from jax.sharding import PartitionSpec as P

DIAG = 2
HOPS = 1
ITERS = 3
AXES = ("lsec", "rsec")
eps = 1e-06
SHIFT = 1.75
SHRINK = 8.0


def shift_blocks(block, down, right):
    rows, cols = lax.axis_size("lsec"), lax.axis_size("rsec")
    pairs = [
        (row * cols + col, (row + down) * cols + col + right)
        for row in range(rows)
        for col in range(cols)
        if 0 <= row + down < rows and 0 <= col + right < cols
    ]
    return lax.ppermute(block, AXES, pairs)


def add_terms(left_env, right_env, source, first, number, total):
    for term in range(first, first + number):
        inner = jnp.einsum(
            "aij,abjk->abik", left_env[:, term], source, preferred_element_type=jnp.float32
        ).astype(jnp.bfloat16)
        total = total + jnp.einsum(
            "abik,blk->abil", inner, right_env[:, term], preferred_element_type=jnp.float32
        )
    return total


def matvec(vec, left_env, right_env, energies):
    total = energies[:, :, None, None] * vec.astype(jnp.float32)
    total = add_terms(left_env, right_env, vec, 0, DIAG, total)
    from_right = shift_blocks(vec[:-1, :1], 0, -1)
    from_left = shift_blocks(vec[1:, -1:], 0, 1)
    from_up = shift_blocks(vec[-1:, 1:], 1, 0)
    from_down = shift_blocks(vec[:1, :-1], -1, 0)
    up_right = shift_blocks(vec[-1:, :1], 1, -1)
    down_left = shift_blocks(vec[:1, -1:], -1, 1)
    plus_blocks = jnp.concatenate(
        [
            jnp.concatenate([from_up, up_right], axis=1),
            jnp.concatenate([vec[:-1, 1:], from_right], axis=1),
        ],
        axis=0,
    )
    minus_blocks = jnp.concatenate(
        [
            jnp.concatenate([from_left, vec[1:, :-1]], axis=1),
            jnp.concatenate([down_left, from_down], axis=1),
        ],
        axis=0,
    )
    total = add_terms(left_env, right_env, plus_blocks, DIAG, HOPS, total)
    total = add_terms(left_env, right_env, minus_blocks, DIAG + HOPS, HOPS, total)
    return total


def coefficient(coef_num, coef_den, step):
    if step == 0:
        return jnp.float32(0.0)
    return coef_num[step - 1].astype(jnp.float32) / coef_den[step - 1].astype(jnp.float32)


def stepwise(psi, left_env, right_env, energies, coef_num, coef_den, count):
    start_vals = psi.astype(jnp.float32)
    start = lax.psum(jnp.sum(start_vals * start_vals), AXES) * count
    vec = (start_vals * lax.rsqrt(start + eps)).astype(jnp.bfloat16)
    previous = jnp.zeros(psi.shape, jnp.float32)
    thetas = []
    for step in range(ITERS):
        sigma = matvec(vec, left_env, right_env, energies)
        vals = vec.astype(jnp.float32)
        coef = coefficient(coef_num, coef_den, step)
        theta = lax.psum(jnp.sum(vals * sigma), AXES) * count
        resid = sigma - theta * vals - coef * previous
        norm_sq = lax.psum(jnp.sum(resid * resid), AXES) * count
        thetas.append(theta)
        previous = vals
        vec = (resid * lax.rsqrt(norm_sq + eps)).astype(jnp.bfloat16)
    return (vec, jnp.stack(thetas))


ROWS, COLS, BLOCKS = 4, 2, 8
SUMS = 10
VMEM = pl.BlockSpec(memory_space=pltpu.VMEM)
SMEM = pl.BlockSpec(memory_space=pltpu.SMEM)
PARAMS = pltpu.CompilerParams(vmem_limit_bytes=40 * 1024 * 1024)


def dot(left, right):
    return lax.dot_general(
        left, right, (((1,), (0,)), ((), ())), preferred_element_type=jnp.float32
    )


def dot_t(left, right):
    return lax.dot_general(
        left, right, (((1,), (1,)), ((), ())), preferred_element_type=jnp.float32
    )


def not_at(place):
    return (lax.axis_index("rsec") != place).astype(jnp.float32)


def masked(block, keep):
    return (block.astype(jnp.float32) * keep).astype(jnp.bfloat16)


def pack_kernel(last, psi_ref, right_ref, energy_ref, pack_ref, left_out, up_out, corner_out, low_out):
    size = psi_ref.shape[-1]
    inner = not_at(last)
    for place in range(2):
        pack_ref[place * size : (place + 1) * size] = masked(psi_ref[place + 1, 1], inner)
        left_out[place] = psi_ref[place, 0]
    pack_ref[2 * size : 3 * size] = psi_ref[3, 1]
    for term in range(4):
        pack_ref[(3 + term) * size : (4 + term) * size] = right_ref[1, term]
    rest = jnp.full((16, size), energy_ref[3, 1], jnp.float32)
    for place in range(3):
        part = rest.astype(jnp.bfloat16)
        start = 7 * size + 16 * place
        pack_ref[start : start + 16] = part
        rest = rest - part.astype(jnp.float32)
    up_out[0] = psi_ref[3, 1]
    corner_out[0] = psi_ref[3, 0]
    low_out[0] = psi_ref[0, 0]
    low_out[1] = masked(psi_ref[0, 1], inner)


def place_in(row, lane, value):
    lanes = lax.broadcasted_iota(jnp.int32, row.shape, row.ndim - 1)
    return jnp.where(lanes == lane, value, row)


def step_kernel(step, last, *refs):
    energy_ref, left_ref, right_ref, psi_ref, pack_ref, *refs = refs
    size = psi_ref.shape[-1]
    if step == 0:
        from_right, from_up, from_corner, from_low, *refs = refs
    else:
        sums_in, *refs = refs
        vecs, refs = refs[:step], refs[step:]
        from_right, from_left, from_top, from_low, *refs = refs
    if step < ITERS - 1:
        new_ref, to_left, to_right, to_top, to_low, sums_ref = refs
    else:
        new_ref, back_ref, sums_ref = refs
    first_keep, last_keep = not_at(0), not_at(last)

    def start_block(k):
        if k == 6:
            return pack_ref[2 * size : 3 * size]
        return psi_ref[k // 2, k % 2] if k < 6 else psi_ref[3, 0]

    def own(k):
        return start_block(k) if step == 0 else vecs[-1][k]

    def left_halo(place):
        return pack_ref[place * size : (place + 1) * size] if step == 0 else from_left[place]

    def top_halo(place):
        if step == 0:
            return (from_up, from_corner)[place][0]
        return from_top[place]

    def sources(k):
        plus = {0: lambda: top_halo(0), 1: lambda: top_halo(1), 2: lambda: own(1), 3: lambda: from_right[0],
                4: lambda: own(3), 5: lambda: from_right[1], 6: lambda: own(4), 7: lambda: own(5)}[k]()
        minus = {0: lambda: left_halo(0), 1: lambda: own(2), 2: lambda: left_halo(1), 3: lambda: own(4),
                 4: lambda: own(6), 5: lambda: own(7), 6: lambda: from_low[0], 7: lambda: from_low[1]}[k]()
        return [own(k)] * DIAG + [plus, minus]

    def right_block(k, term):
        if k == 6:
            return pack_ref[(3 + term) * size : (4 + term) * size]
        return right_ref[k % 2 if k < 6 else 0, term]

    totals = [jnp.zeros((8, size), jnp.float32) for _ in range(step + 2 + (step == 0))]

    def add_product(place, one, other):
        product = one * other
        totals[place] = totals[place] + jnp.sum(product.reshape(size // 8, 8, size), axis=0)

    for k in range(BLOCKS):
        if k == 6:
            energy = sum(
                pack_ref[7 * size + 16 * place : 7 * size + 16 * place + 16].astype(jnp.float32)
                for place in range(3)
            )[:1]
        else:
            energy = energy_ref[k // 2, k % 2] if k < 6 else energy_ref[3, 0]
        total = (energy - SHIFT) * own(k).astype(jnp.float32)
        for term, source in enumerate(sources(k)):
            inner = dot(left_ref[k // 2, term], source)
            if (k, term) in ((6, DIAG), (4, DIAG + HOPS)):
                inner = inner * first_keep
            total = total + dot_t(inner.astype(jnp.bfloat16), right_block(k, term))
        image = total.astype(jnp.bfloat16)
        new_ref[k] = image
        vals = image.astype(jnp.float32)
        start_vals = start_block(k).astype(jnp.float32)
        if step == 0:
            add_product(0, start_vals, start_vals)
            add_product(1, start_vals, vals)
            add_product(2, vals, vals)
        else:
            add_product(0, start_vals, vals)
            for place, vec in enumerate(vecs):
                add_product(place + 1, vec[k].astype(jnp.float32), vals)
            add_product(step + 1, vals, vals)
        if step < ITERS - 1:
            for place, out, slot, keep in (
                (0, to_left, 0, None), (2, to_left, 1, None), (3, to_right, 0, None), (5, to_right, 1, None),
                (6, to_top, 0, None), (7, to_top, 1, first_keep), (0, to_low, 0, None), (1, to_low, 1, last_keep),
            ):
                if place == k:
                    out[slot] = image if keep is None else masked(image, keep)
        elif k == 6:
            for place, vec in enumerate(vecs):
                back_ref[place] = vec[k]
            back_ref[step] = image
    row = jnp.zeros((1, 128), jnp.float32) if step == 0 else sums_in[0:1]
    start = {0: 0, 1: 3, 2: 6}[step]
    for place, total in enumerate(totals):
        value = jnp.sum(jnp.sum(total, axis=0, keepdims=True), axis=1, keepdims=True)
        row = place_in(row, start + place, value)
    sums_ref[...] = jnp.broadcast_to(row, sums_ref.shape)


def recursion(gram, coefs):
    def quad(left, right):
        return sum(
            left[i] * right[j] * gram[min(i, j)][max(i, j)]
            for i in range(len(left))
            for j in range(len(right))
        )

    scale = lax.rsqrt(gram[0][0] + eps)
    vec, previous = [scale], []
    thetas, fine = [], jnp.ones_like(scale)
    for step in range(ITERS):
        moved = [jnp.zeros_like(scale)] + vec
        theta = quad(vec, [SHIFT * entry for entry in vec]) + quad(vec, moved)
        thetas.append(theta)
        resid = list(moved)
        for i, entry in enumerate(vec):
            resid[i] = resid[i] + (SHIFT - theta) * entry
        for i, entry in enumerate(previous):
            resid[i] = resid[i] - coefs[step] * entry
        norm_sq = quad(resid, resid)
        lead = resid[-1]
        held = lead * lead * gram[step + 1][step + 1] <= SHRINK * (norm_sq + eps)
        fine = jnp.where(held, fine, 0.0)
        norm = lax.rsqrt(jnp.maximum(norm_sq, 0.0) + eps)
        previous = vec
        vec = [entry * norm for entry in resid]
    return vec, thetas, fine


def combine_kernel(count, num_ref, den_ref, sums_ref, psi_ref, one_ref, two_ref, three_ref, back_ref, out_ref, row_ref):
    sums = jnp.sum(sums_ref[...], axis=0, keepdims=True) * count
    lanes = lax.broadcasted_iota(jnp.int32, sums.shape, 1)
    entries = [
        jnp.sum(jnp.where(lanes == place, sums, 0.0), axis=1, keepdims=True) for place in range(SUMS)
    ]
    gram = [[None] * (ITERS + 1) for _ in range(ITERS + 1)]
    place = 0
    for right in range(ITERS + 1):
        for left in range(right + 1):
            gram[left][right] = entries[place]
            place += 1
    coefs = [jnp.zeros_like(entries[0])]
    for step in range(ITERS - 1):
        num = jnp.full(entries[0].shape, num_ref[step], jnp.int32).astype(jnp.float32)
        den = jnp.full(entries[0].shape, den_ref[step], jnp.int32).astype(jnp.float32)
        coefs.append(num / den)
    weights, thetas, fine = recursion(gram, coefs)
    row = jnp.zeros((1, 128), jnp.float32)
    for place, value in enumerate(thetas + [fine]):
        row = place_in(row, place, value)
    row_ref[...] = row
    for i in range(ROWS):
        for j in range(COLS):
            k = 2 * i + j + (i == 3)
            blocks = [psi_ref[i, j]]
            if k == 8:
                blocks += [back_ref[0], back_ref[1], back_ref[2]]
            else:
                blocks += [one_ref[k], two_ref[k], three_ref[k]]
            total = weights[0] * blocks[0].astype(jnp.float32)
            for weight, block in zip(weights[1:], blocks[1:]):
                total = total + weight * block.astype(jnp.float32)
            out_ref[i, j] = total.astype(jnp.bfloat16)


def move(block, down, right, around):
    rows, cols = lax.axis_size("lsec"), lax.axis_size("rsec")
    pairs = [
        (row * cols + col, (row + down) * cols + (col + right) % cols)
        for row in range(rows)
        for col in range(cols)
        if 0 <= row + down < rows and (around or 0 <= col + right < cols)
    ]
    return lax.ppermute(block, AXES, pairs)


def call(kernel, in_specs, out_shapes, flops, *args):
    nbytes = sum(a.size * a.dtype.itemsize for a in args)
    nbytes += sum(s.size * s.dtype.itemsize for s in out_shapes)
    return pl.pallas_call(
        kernel,
        in_specs=in_specs,
        out_specs=[VMEM] * len(out_shapes),
        out_shape=out_shapes,
        compiler_params=PARAMS,
        cost_estimate=pl.CostEstimate(flops=flops, bytes_accessed=nbytes, transcendentals=0),
    )(*args)


def per_device(psi, left_env, right_env, energies, coef_num, coef_den):
    size = psi.shape[-1]
    devices = lax.axis_size("lsec") * lax.axis_size("rsec")
    last = lax.axis_size("rsec") - 1
    count = 1.0 / float(psi.size * devices)

    def blocks(number):
        return jax.ShapeDtypeStruct((number, size, size), jnp.bfloat16)

    pack, to_left, to_up, to_corner, to_low = call(
        lambda *refs: pack_kernel(last, *refs),
        [VMEM, VMEM, SMEM],
        [jax.ShapeDtypeStruct((7 * size + 48, size), jnp.bfloat16), blocks(2), blocks(1), blocks(1), blocks(2)],
        0, psi, right_env, energies,
    )
    pack = move(pack, 0, 1, True)
    halos = [
        move(to_left, 0, -1, False),
        move(to_up, 1, 0, False),
        move(to_corner, 1, -1, False),
        move(to_low, -1, 1, True),
    ]
    fixed = [energies, left_env, right_env, psi, pack]
    vecs, sums = [], []
    for step in range(ITERS):
        final = step == ITERS - 1
        row = jax.ShapeDtypeStruct((devices if final else 8, 128), jnp.float32)
        outs = [blocks(BLOCKS), blocks(ITERS), row] if final else [blocks(BLOCKS)] + [blocks(2)] * 4 + [row]
        ins = fixed + sums + vecs + halos
        result = call(
            lambda *refs, step=step: step_kernel(step, last, *refs),
            [SMEM] + [VMEM] * (len(ins) - 1), outs, 2 * 64 * size**3, *ins,
        )
        vecs.append(result[0])
        sums = [result[-1]]
        if not final:
            to_left, to_right, to_top, to_low = result[1:5]
            halos = [
                move(to_left, 0, -1, False),
                move(to_right, 0, 1, False),
                move(to_top, 1, -1, True),
                move(to_low, -1, 1, True),
            ]
    back = move(result[1], 0, -1, True)
    gathered = lax.all_to_all(sums[0].reshape(devices, 1, 128), AXES, 0, 0).reshape(devices, 128)
    vec, row = call(
        lambda *refs: combine_kernel(count, *refs),
        [SMEM, SMEM] + [VMEM] * 6,
        [jax.ShapeDtypeStruct(psi.shape, jnp.bfloat16), jax.ShapeDtypeStruct((1, 128), jnp.float32)],
        0, coef_num, coef_den, gathered, psi, *vecs, back,
    )
    thetas = row[0, :ITERS]
    return lax.cond(
        row[0, ITERS] > 0.5,
        lambda: (vec, thetas),
        lambda: stepwise(psi, left_env, right_env, energies, coef_num, coef_den, count),
    )


def solution(mesh):
    in_specs = (
        P("lsec", "rsec", None, None),
        P("lsec", None, None, None),
        P("rsec", None, None, None),
        P("lsec", "rsec"),
        P(),
        P(),
    )
    out_specs = (P("lsec", "rsec", None, None), P())
    return jax.shard_map(
        per_device, mesh=mesh, in_specs=in_specs, out_specs=out_specs, check_vma=False
    )
```

```python
import jax
import jax.numpy as jnp
from jax import lax
from jax.experimental import pallas as pl
from jax.experimental.pallas import tpu as pltpu
from jax.sharding import PartitionSpec as P

DIAG = 2
HOPS = 1
ITERS = 3
AXES = ("lsec", "rsec")
eps = 1e-06
SHIFT = 1.75
SHRINK = 8.0


def shift_blocks(block, down, right):
    rows, cols = lax.axis_size("lsec"), lax.axis_size("rsec")
    pairs = [
        (row * cols + col, (row + down) * cols + col + right)
        for row in range(rows)
        for col in range(cols)
        if 0 <= row + down < rows and 0 <= col + right < cols
    ]
    return lax.ppermute(block, AXES, pairs)


def add_terms(left_env, right_env, source, first, number, total):
    for term in range(first, first + number):
        inner = jnp.einsum(
            "aij,abjk->abik", left_env[:, term], source, preferred_element_type=jnp.float32
        ).astype(jnp.bfloat16)
        total = total + jnp.einsum(
            "abik,blk->abil", inner, right_env[:, term], preferred_element_type=jnp.float32
        )
    return total


def matvec(vec, left_env, right_env, energies):
    total = energies[:, :, None, None] * vec.astype(jnp.float32)
    total = add_terms(left_env, right_env, vec, 0, DIAG, total)
    from_right = shift_blocks(vec[:-1, :1], 0, -1)
    from_left = shift_blocks(vec[1:, -1:], 0, 1)
    from_up = shift_blocks(vec[-1:, 1:], 1, 0)
    from_down = shift_blocks(vec[:1, :-1], -1, 0)
    up_right = shift_blocks(vec[-1:, :1], 1, -1)
    down_left = shift_blocks(vec[:1, -1:], -1, 1)
    plus_blocks = jnp.concatenate(
        [
            jnp.concatenate([from_up, up_right], axis=1),
            jnp.concatenate([vec[:-1, 1:], from_right], axis=1),
        ],
        axis=0,
    )
    minus_blocks = jnp.concatenate(
        [
            jnp.concatenate([from_left, vec[1:, :-1]], axis=1),
            jnp.concatenate([down_left, from_down], axis=1),
        ],
        axis=0,
    )
    total = add_terms(left_env, right_env, plus_blocks, DIAG, HOPS, total)
    total = add_terms(left_env, right_env, minus_blocks, DIAG + HOPS, HOPS, total)
    return total


def coefficient(coef_num, coef_den, step):
    if step == 0:
        return jnp.float32(0.0)
    return coef_num[step - 1].astype(jnp.float32) / coef_den[step - 1].astype(jnp.float32)


def stepwise(psi, left_env, right_env, energies, coef_num, coef_den, count):
    start_vals = psi.astype(jnp.float32)
    start = lax.psum(jnp.sum(start_vals * start_vals), AXES) * count
    vec = (start_vals * lax.rsqrt(start + eps)).astype(jnp.bfloat16)
    previous = jnp.zeros(psi.shape, jnp.float32)
    thetas = []
    for step in range(ITERS):
        sigma = matvec(vec, left_env, right_env, energies)
        vals = vec.astype(jnp.float32)
        coef = coefficient(coef_num, coef_den, step)
        theta = lax.psum(jnp.sum(vals * sigma), AXES) * count
        resid = sigma - theta * vals - coef * previous
        norm_sq = lax.psum(jnp.sum(resid * resid), AXES) * count
        thetas.append(theta)
        previous = vals
        vec = (resid * lax.rsqrt(norm_sq + eps)).astype(jnp.bfloat16)
    return (vec, jnp.stack(thetas))


ROWS, COLS, BLOCKS = 4, 2, 8
SUMS = 10
VMEM = pl.BlockSpec(memory_space=pltpu.VMEM)
SMEM = pl.BlockSpec(memory_space=pltpu.SMEM)
PARAMS = pltpu.CompilerParams(vmem_limit_bytes=40 * 1024 * 1024)


def dot(left, right):
    return lax.dot_general(
        left, right, (((1,), (0,)), ((), ())), preferred_element_type=jnp.float32
    )


def dot_t(left, right):
    return lax.dot_general(
        left, right, (((1,), (1,)), ((), ())), preferred_element_type=jnp.float32
    )


def not_at(place):
    return (lax.axis_index("rsec") != place).astype(jnp.float32)


def masked(block, keep):
    return (block.astype(jnp.float32) * keep).astype(jnp.bfloat16)


def pack_kernel(last, psi_ref, right_ref, energy_ref, pack_ref, left_out, up_out, corner_out, low_out):
    size = psi_ref.shape[-1]
    inner = not_at(last)
    for place in range(2):
        pack_ref[place * size : (place + 1) * size] = masked(psi_ref[place + 1, 1], inner)
        left_out[place] = psi_ref[place, 0]
    pack_ref[2 * size : 3 * size] = psi_ref[3, 1]
    for term in range(4):
        pack_ref[(3 + term) * size : (4 + term) * size] = right_ref[1, term]
    rest = jnp.full((16, size), energy_ref[1, 3], jnp.float32)
    for place in range(3):
        part = rest.astype(jnp.bfloat16)
        start = 7 * size + 16 * place
        pack_ref[start : start + 16] = part
        rest = rest - part.astype(jnp.float32)
    up_out[0] = psi_ref[3, 1]
    corner_out[0] = psi_ref[3, 0]
    low_out[0] = psi_ref[0, 0]
    low_out[1] = masked(psi_ref[0, 1], inner)


def place_in(row, lane, value):
    lanes = lax.broadcasted_iota(jnp.int32, row.shape, row.ndim - 1)
    return jnp.where(lanes == lane, value, row)


class Blocks:
    def __init__(self, step, psi_ref, pack_ref, vec_ref, halo_refs):
        self.step, self.psi_ref, self.pack_ref, self.vec_ref = step, psi_ref, pack_ref, vec_ref
        self.size = psi_ref.shape[-1]
        self.halo_refs = halo_refs

    def packed(self, place):
        return self.pack_ref[place * self.size : (place + 1) * self.size]

    def start(self, k):
        if k == 6:
            return self.packed(2)
        return self.psi_ref[k // 2, k % 2] if k < 6 else self.psi_ref[3, 0]

    def own(self, k):
        return self.start(k) if self.step == 0 else self.vec_ref[k]

    def source(self, k, term):
        if term < DIAG:
            return self.own(k)
        if term == DIAG:
            halo = {0: (0, 0), 1: (0, 1), 3: (3, 0), 5: (3, 1)}
            inside = {2: 1, 4: 3, 6: 4, 7: 5}
        else:
            halo = {0: (2, 0), 2: (2, 1), 6: (1, 0), 7: (1, 1)}
            inside = {1: 2, 3: 4, 4: 6, 5: 7}
        if k in inside:
            return self.own(inside[k])
        group, place = halo[k]
        if self.step == 0 and group == 0:
            return self.halo_refs[(0, 4)[place]][0]
        if self.step == 0 and group == 2:
            return self.packed(place)
        return self.halo_refs[group][place]

    def near(self, k, term):
        if self.step == 0 and (k == 6 or (k, term) == (4, DIAG + HOPS)):
            return False
        if term < DIAG:
            return True
        return k in ((2, 4, 6, 7) if term == DIAG else (1, 3, 4, 5))

    def term(self, k, term, left_ref, right_ref, first_keep):
        inner = dot(left_ref[k // 2, term], self.source(k, term))
        if (k, term) in ((6, DIAG), (4, DIAG + HOPS)):
            inner = inner * first_keep
        right = self.packed(3 + term) if k == 6 else right_ref[k % 2 if k < 6 else 0, term]
        return dot_t(inner.astype(jnp.bfloat16), right)

    def energy(self, k, energy_ref):
        if k == 6:
            start = 7 * self.size
            parts = [self.pack_ref[start + 16 * i : start + 16 * i + 16].astype(jnp.float32) for i in range(3)]
            return sum(parts)[:1] - SHIFT
        return (energy_ref[k % 2, k // 2] if k < 6 else energy_ref[0, 3]) - SHIFT


class Sums:
    def __init__(self, number, size):
        self.size = size
        self.totals = [jnp.zeros((8, size), jnp.float32) for _ in range(number)]

    def add(self, place, one, other):
        product = (one * other).reshape(self.size // 8, 8, self.size)
        self.totals[place] = self.totals[place] + jnp.sum(product, axis=0)

    def write(self, row, first):
        for place, total in enumerate(self.totals):
            value = jnp.sum(jnp.sum(total, axis=0, keepdims=True), axis=1, keepdims=True)
            row = place_in(row, first + place, value)
        return row


FIRST_SUM = (0, 1, 3, 6)


def near_kernel(step, *refs):
    energy_ref, left_ref, right_ref, psi_ref, *refs = refs
    if step == 0:
        pack_ref, vecs, refs = None, [], refs
    else:
        pack_ref, *refs = refs
        sums_in, *refs = refs
        vecs, refs = refs[:step], refs[step:]
    total_ref, sums_ref = refs
    blocks = Blocks(step, psi_ref, pack_ref, vecs[-1] if vecs else None, ())
    first_keep = not_at(0)
    sums = Sums(step + 1, blocks.size)
    for k in range(BLOCKS):
        terms = [term for term in range(4) if blocks.near(k, term)]
        if not terms:
            continue
        own = blocks.own(k).astype(jnp.float32)
        total = blocks.energy(k, energy_ref) * own
        for term in terms:
            total = total + blocks.term(k, term, left_ref, right_ref, first_keep)
        total_ref[k] = total
    for k in range(BLOCKS):
        if step == 0:
            vals = psi_ref[k // 2, k % 2].astype(jnp.float32)
            sums.add(0, vals, vals)
            continue
        own = blocks.own(k).astype(jnp.float32)
        sums.add(0, blocks.start(k).astype(jnp.float32), own)
        for place, vec in enumerate(vecs[:-1]):
            sums.add(place + 1, vec[k].astype(jnp.float32), own)
        sums.add(step, own, own)
    row = jnp.zeros((1, 128), jnp.float32) if step == 0 else sums_in[0:1]
    sums_ref[...] = jnp.broadcast_to(sums.write(row, FIRST_SUM[step]), sums_ref.shape)


def far_kernel(step, last, *refs):
    energy_ref, left_ref, right_ref, psi_ref, pack_ref, total_ref, *refs = refs
    final = step == ITERS - 1
    if final:
        sums_in, *refs = refs
        vecs, refs = refs[:step], refs[step:]
    elif step > 0:
        vecs, refs = refs[:1], refs[1:]
    else:
        vecs = []
    halos = 4
    halo_refs, refs = refs[:halos], refs[halos:]
    if step == 0:
        up, low, left, corner = halo_refs
        halo_refs = (up, low, None, left, corner)
    blocks = Blocks(step, psi_ref, pack_ref, vecs[-1] if vecs else None, halo_refs)
    first_keep, last_keep = not_at(0), not_at(last)
    if final:
        new_ref, back_ref, sums_ref = refs
        sums = Sums(step + 2, blocks.size)
    else:
        new_ref, to_top, to_low, to_left, to_right = refs
    for k in (0, 1, 6, 7, 2, 3, 4, 5):
        far = [term for term in range(4) if not blocks.near(k, term)]
        if len(far) == 4:
            total = blocks.energy(k, energy_ref) * blocks.own(k).astype(jnp.float32)
        else:
            total = total_ref[k]
        for term in far:
            total = total + blocks.term(k, term, left_ref, right_ref, first_keep)
        image = total.astype(jnp.bfloat16)
        new_ref[k] = image
        if final:
            vals = image.astype(jnp.float32)
            sums.add(0, blocks.start(k).astype(jnp.float32), vals)
            for place, vec in enumerate(vecs):
                sums.add(place + 1, vec[k].astype(jnp.float32), vals)
            sums.add(step + 1, vals, vals)
            if k == 6:
                for place, vec in enumerate(vecs):
                    back_ref[place] = vec[k]
                back_ref[step] = image
            continue
        for place, out, slot, keep in (
            (0, to_left, 0, None), (2, to_left, 1, None), (3, to_right, 0, None), (5, to_right, 1, None),
            (6, to_top, 0, None), (7, to_top, 1, first_keep), (0, to_low, 0, None), (1, to_low, 1, last_keep),
        ):
            if place == k:
                out[slot] = image if keep is None else masked(image, keep)
    if final:
        row = sums.write(sums_in[0:1], FIRST_SUM[ITERS])
        sums_ref[...] = jnp.broadcast_to(row, sums_ref.shape)


def recursion(gram, coefs):
    def quad(left, right):
        return sum(
            left[i] * right[j] * gram[min(i, j)][max(i, j)]
            for i in range(len(left))
            for j in range(len(right))
        )

    scale = lax.rsqrt(gram[0][0] + eps)
    vec, previous = [scale], []
    thetas, fine = [], jnp.ones_like(scale)
    for step in range(ITERS):
        moved = [jnp.zeros_like(scale)] + vec
        theta = quad(vec, [SHIFT * entry for entry in vec]) + quad(vec, moved)
        thetas.append(theta)
        resid = list(moved)
        for i, entry in enumerate(vec):
            resid[i] = resid[i] + (SHIFT - theta) * entry
        for i, entry in enumerate(previous):
            resid[i] = resid[i] - coefs[step] * entry
        norm_sq = quad(resid, resid)
        lead = resid[-1]
        held = lead * lead * gram[step + 1][step + 1] <= SHRINK * (norm_sq + eps)
        fine = jnp.where(held, fine, 0.0)
        norm = lax.rsqrt(jnp.maximum(norm_sq, 0.0) + eps)
        previous = vec
        vec = [entry * norm for entry in resid]
    return vec, thetas, fine


def combine_kernel(count, num_ref, den_ref, sums_ref, psi_ref, one_ref, two_ref, three_ref, back_ref, out_ref, row_ref):
    sums = jnp.sum(sums_ref[...], axis=0, keepdims=True) * count
    lanes = lax.broadcasted_iota(jnp.int32, sums.shape, 1)
    entries = [
        jnp.sum(jnp.where(lanes == place, sums, 0.0), axis=1, keepdims=True) for place in range(SUMS)
    ]
    gram = [[None] * (ITERS + 1) for _ in range(ITERS + 1)]
    place = 0
    for right in range(ITERS + 1):
        for left in range(right + 1):
            gram[left][right] = entries[place]
            place += 1
    coefs = [jnp.zeros_like(entries[0])]
    for step in range(ITERS - 1):
        num = jnp.full(entries[0].shape, num_ref[step], jnp.int32).astype(jnp.float32)
        den = jnp.full(entries[0].shape, den_ref[step], jnp.int32).astype(jnp.float32)
        coefs.append(num / den)
    weights, thetas, fine = recursion(gram, coefs)
    row = jnp.zeros((1, 128), jnp.float32)
    for place, value in enumerate(thetas + [fine]):
        row = place_in(row, place, value)
    row_ref[...] = row
    for i in range(ROWS):
        for j in range(COLS):
            k = 2 * i + j + (i == 3)
            blocks = [psi_ref[i, j]]
            if k == 8:
                blocks += [back_ref[0], back_ref[1], back_ref[2]]
            else:
                blocks += [one_ref[k], two_ref[k], three_ref[k]]
            total = weights[0] * blocks[0].astype(jnp.float32)
            for weight, block in zip(weights[1:], blocks[1:]):
                total = total + weight * block.astype(jnp.float32)
            out_ref[i, j] = total.astype(jnp.bfloat16)


def move(block, down, right, around):
    rows, cols = lax.axis_size("lsec"), lax.axis_size("rsec")
    pairs = [
        (row * cols + col, (row + down) * cols + (col + right) % cols)
        for row in range(rows)
        for col in range(cols)
        if 0 <= row + down < rows and (around or 0 <= col + right < cols)
    ]
    return lax.ppermute(block, AXES, pairs)


def call(kernel, in_specs, out_shapes, flops, *args):
    nbytes = sum(a.size * a.dtype.itemsize for a in args)
    nbytes += sum(s.size * s.dtype.itemsize for s in out_shapes)
    return pl.pallas_call(
        kernel,
        in_specs=in_specs,
        out_specs=[VMEM] * len(out_shapes),
        out_shape=out_shapes,
        compiler_params=PARAMS,
        cost_estimate=pl.CostEstimate(flops=flops, bytes_accessed=nbytes, transcendentals=0),
    )(*args)


def per_device(psi, left_env, right_env, energies, coef_num, coef_den):
    size = psi.shape[-1]
    devices = lax.axis_size("lsec") * lax.axis_size("rsec")
    last = lax.axis_size("rsec") - 1
    count = 1.0 / float(psi.size * devices)

    def blocks(number):
        return jax.ShapeDtypeStruct((number, size, size), jnp.bfloat16)

    levels = energies.T
    pack, to_left, to_up, to_corner, to_low = call(
        lambda *refs: pack_kernel(last, *refs),
        [VMEM, VMEM, SMEM],
        [jax.ShapeDtypeStruct((7 * size + 48, size), jnp.bfloat16), blocks(2), blocks(1), blocks(1), blocks(2)],
        0, psi, right_env, levels,
    )
    pack = move(pack, 0, 1, True)
    to_low = move(to_low, -1, 1, True)
    to_up = move(to_up, 1, 0, False)
    to_corner = move(to_corner, 1, -1, False)
    to_left = move(to_left, 0, -1, False)
    halos = [to_up, to_low, to_left, to_corner]
    fixed = [levels, left_env, right_env, psi]
    row = jax.ShapeDtypeStruct((8, 128), jnp.float32)
    vecs, sums = [], []
    for step in range(ITERS):
        final = step == ITERS - 1
        ins = fixed + ([pack] + sums + vecs if step else [])
        partial, *sums = call(
            lambda *refs, step=step: near_kernel(step, *refs),
            [SMEM] + [VMEM] * (len(ins) - 1),
            [jax.ShapeDtypeStruct((BLOCKS, size, size), jnp.float32), row],
            4 * (24 if step else 20) * size**3, *ins,
        )
        ins = fixed + [pack, partial] + (sums + vecs if final else vecs[-1:]) + halos
        if final:
            outs = [blocks(BLOCKS), blocks(ITERS), jax.ShapeDtypeStruct((devices, 128), jnp.float32)]
        else:
            outs = [blocks(BLOCKS)] + [blocks(2)] * 4
        result = call(
            lambda *refs, step=step: far_kernel(step, last, *refs),
            [SMEM] + [VMEM] * (len(ins) - 1), outs, 4 * (8 if step else 12) * size**3, *ins,
        )
        vecs.append(result[0])
        if not final:
            to_top, to_low, to_left, to_right = result[1:5]
            to_top = move(to_top, 1, -1, True)
            to_low = move(to_low, -1, 1, True)
            to_left = move(to_left, 0, -1, False)
            to_right = move(to_right, 0, 1, False)
            halos = [to_top, to_low, to_right, to_left]
    sums = [result[-1]]
    back = move(result[1], 0, -1, True)
    gathered = lax.all_to_all(sums[0].reshape(devices, 1, 128), AXES, 0, 0).reshape(devices, 128)
    vec, row = call(
        lambda *refs: combine_kernel(count, *refs),
        [SMEM, SMEM] + [VMEM] * 6,
        [jax.ShapeDtypeStruct(psi.shape, jnp.bfloat16), jax.ShapeDtypeStruct((1, 128), jnp.float32)],
        0, coef_num, coef_den, gathered, psi, *vecs, back,
    )
    thetas = row[0, :ITERS]
    return lax.cond(
        row[0, ITERS] > 0.5,
        lambda: (vec, thetas),
        lambda: stepwise(psi, left_env, right_env, energies, coef_num, coef_den, count),
    )


def solution(mesh):
    in_specs = (
        P("lsec", "rsec", None, None),
        P("lsec", None, None, None),
        P("rsec", None, None, None),
        P("lsec", "rsec"),
        P(),
        P(),
    )
    out_specs = (P("lsec", "rsec", None, None), P())
    return jax.shard_map(
        per_device, mesh=mesh, in_specs=in_specs, out_specs=out_specs, check_vma=False
    )
```

```python
import jax
import jax.numpy as jnp
from jax import lax
from jax.experimental import pallas as pl
from jax.experimental.pallas import tpu as pltpu
from jax.sharding import PartitionSpec as P

DIAG = 2
HOPS = 1
ITERS = 3
AXES = ("lsec", "rsec")
eps = 1e-06
SHIFT = 1.75
SHRINK = 8.0


def shift_blocks(block, down, right):
    rows, cols = lax.axis_size("lsec"), lax.axis_size("rsec")
    pairs = [
        (row * cols + col, (row + down) * cols + col + right)
        for row in range(rows)
        for col in range(cols)
        if 0 <= row + down < rows and 0 <= col + right < cols
    ]
    return lax.ppermute(block, AXES, pairs)


def add_terms(left_env, right_env, source, first, number, total):
    for term in range(first, first + number):
        inner = jnp.einsum(
            "aij,abjk->abik", left_env[:, term], source, preferred_element_type=jnp.float32
        ).astype(jnp.bfloat16)
        total = total + jnp.einsum(
            "abik,blk->abil", inner, right_env[:, term], preferred_element_type=jnp.float32
        )
    return total


def matvec(vec, left_env, right_env, energies):
    total = energies[:, :, None, None] * vec.astype(jnp.float32)
    total = add_terms(left_env, right_env, vec, 0, DIAG, total)
    from_right = shift_blocks(vec[:-1, :1], 0, -1)
    from_left = shift_blocks(vec[1:, -1:], 0, 1)
    from_up = shift_blocks(vec[-1:, 1:], 1, 0)
    from_down = shift_blocks(vec[:1, :-1], -1, 0)
    up_right = shift_blocks(vec[-1:, :1], 1, -1)
    down_left = shift_blocks(vec[:1, -1:], -1, 1)
    plus_blocks = jnp.concatenate(
        [
            jnp.concatenate([from_up, up_right], axis=1),
            jnp.concatenate([vec[:-1, 1:], from_right], axis=1),
        ],
        axis=0,
    )
    minus_blocks = jnp.concatenate(
        [
            jnp.concatenate([from_left, vec[1:, :-1]], axis=1),
            jnp.concatenate([down_left, from_down], axis=1),
        ],
        axis=0,
    )
    total = add_terms(left_env, right_env, plus_blocks, DIAG, HOPS, total)
    total = add_terms(left_env, right_env, minus_blocks, DIAG + HOPS, HOPS, total)
    return total


def coefficient(coef_num, coef_den, step):
    if step == 0:
        return jnp.float32(0.0)
    return coef_num[step - 1].astype(jnp.float32) / coef_den[step - 1].astype(jnp.float32)


def stepwise(psi, left_env, right_env, energies, coef_num, coef_den, count):
    start_vals = psi.astype(jnp.float32)
    start = lax.psum(jnp.sum(start_vals * start_vals), AXES) * count
    vec = (start_vals * lax.rsqrt(start + eps)).astype(jnp.bfloat16)
    previous = jnp.zeros(psi.shape, jnp.float32)
    thetas = []
    for step in range(ITERS):
        sigma = matvec(vec, left_env, right_env, energies)
        vals = vec.astype(jnp.float32)
        coef = coefficient(coef_num, coef_den, step)
        theta = lax.psum(jnp.sum(vals * sigma), AXES) * count
        resid = sigma - theta * vals - coef * previous
        norm_sq = lax.psum(jnp.sum(resid * resid), AXES) * count
        thetas.append(theta)
        previous = vals
        vec = (resid * lax.rsqrt(norm_sq + eps)).astype(jnp.bfloat16)
    return (vec, jnp.stack(thetas))


ROWS, COLS, BLOCKS = 4, 2, 8
SUMS = 10
VMEM = pl.BlockSpec(memory_space=pltpu.VMEM)
SMEM = pl.BlockSpec(memory_space=pltpu.SMEM)
PARAMS = pltpu.CompilerParams(vmem_limit_bytes=40 * 1024 * 1024)


def dot(left, right):
    return lax.dot_general(
        left, right, (((1,), (0,)), ((), ())), preferred_element_type=jnp.float32
    )


def dot_t(left, right):
    return lax.dot_general(
        left, right, (((1,), (1,)), ((), ())), preferred_element_type=jnp.float32
    )


def not_at(place):
    return (lax.axis_index("rsec") != place).astype(jnp.float32)


def masked(block, keep):
    return (block.astype(jnp.float32) * keep).astype(jnp.bfloat16)


def write_energy(ref, start, value):
    rest = jnp.full((16, ref.shape[-1]), value, jnp.float32)
    for place in range(3):
        part = rest.astype(jnp.bfloat16)
        ref[start + 16 * place : start + 16 * place + 16] = part
        rest = rest - part.astype(jnp.float32)


def pack_kernel(psi_ref, right_ref, energy_ref, right_out, left_out, top_out, low_out, corner_out):
    size = psi_ref.shape[-1]
    for place, (i, j) in enumerate(((2, 1), (3, 0), (3, 1))):
        right_out[place * size : (place + 1) * size] = psi_ref[i, j]
        write_energy(right_out, 11 * size + 48 * place, energy_ref[j, i])
    left_out[:size] = psi_ref[0, 0]
    write_energy(left_out, 5 * size, energy_ref[0, 0])
    for term in range(4):
        for col in range(COLS):
            start = (3 + 4 * col + term) * size
            right_out[start : start + size] = right_ref[col, term]
        left_out[(1 + term) * size : (2 + term) * size] = right_ref[0, term]
    top_out[0] = masked(psi_ref[3, 0], not_at(0))
    top_out[1] = psi_ref[3, 1]
    low_out[0] = psi_ref[0, 1]
    corner_out[0] = psi_ref[0, 0]


def place_in(row, lane, value):
    lanes = lax.broadcasted_iota(jnp.int32, row.shape, row.ndim - 1)
    return jnp.where(lanes == lane, value, row)


HELD = {0: (0, 1), 2: (1, 0), 3: (1, 1), 5: (2, 0)}
PACKED = {4: 0, 6: 1, 7: 2}
COLUMN = {4: 1, 6: 0, 7: 1}


class Blocks:
    def __init__(self, step, psi_ref, packs, vec_ref, halo_refs, last):
        self.step, self.psi_ref, self.vec_ref, self.halo_refs = step, psi_ref, vec_ref, halo_refs
        self.from_left, self.from_right = packs
        self.size = psi_ref.shape[-1]
        first, last = not_at(0), not_at(last)
        self.cut = {(4, 2): first, (7, 5): first, (3, 1): last}

    def start(self, k):
        if k in HELD:
            return self.psi_ref[HELD[k]]
        if k == 1:
            return self.from_right[: self.size]
        return self.from_left[PACKED[k] * self.size : (PACKED[k] + 1) * self.size]

    def own(self, k):
        return self.start(k) if self.step == 0 else self.vec_ref[k]

    def place(self, k, term):
        return k if term < DIAG else k - 2 if term == DIAG else k + 2

    def source(self, k, term):
        place = self.place(k, term)
        if 0 <= place < BLOCKS:
            return self.own(place)
        top = place < 0
        if self.step == 0 and not top:
            return self.halo_refs[1 + k % 2][0]
        return self.halo_refs[0 if top else 1][k % 2]

    def near(self, k, term):
        place = self.place(k, term)
        if self.step == 0:
            return k in HELD and place in HELD
        return 0 <= place < BLOCKS

    def right(self, k, term, right_ref):
        if k in HELD:
            return right_ref[HELD[k][1], term]
        if k == 1:
            return self.from_right[(1 + term) * self.size : (2 + term) * self.size]
        start = (3 + 4 * COLUMN[k] + term) * self.size
        return self.from_left[start : start + self.size]

    def term(self, k, term, left_ref, right_ref):
        inner = dot(left_ref[k // 2, term], self.source(k, term))
        place = self.place(k, term)
        keep = self.cut.get((max(k, place), min(k, place))) if term >= DIAG else None
        if keep is not None:
            inner = inner * keep
        return dot_t(inner.astype(jnp.bfloat16), self.right(k, term, right_ref))

    def energy(self, k, energy_ref):
        if k in HELD:
            i, j = HELD[k]
            return energy_ref[j, i] - SHIFT
        ref, start = (self.from_right, 5 * self.size) if k == 1 else (self.from_left, 11 * self.size + 48 * PACKED[k])
        parts = [ref[start + 16 * i : start + 16 * i + 16].astype(jnp.float32) for i in range(3)]
        return sum(parts)[:1] - SHIFT


class Sums:
    def __init__(self, number, size):
        self.size = size
        self.totals = [jnp.zeros((8, size), jnp.float32) for _ in range(number)]

    def add(self, place, one, other):
        product = (one * other).reshape(self.size // 8, 8, self.size)
        self.totals[place] = self.totals[place] + jnp.sum(product, axis=0)

    def write(self, row, first):
        for place, total in enumerate(self.totals):
            value = jnp.sum(jnp.sum(total, axis=0, keepdims=True), axis=1, keepdims=True)
            row = place_in(row, first + place, value)
        return row


FIRST_SUM = (0, 1, 3, 6)


def near_kernel(step, last, *refs):
    energy_ref, left_ref, right_ref, psi_ref, *refs = refs
    if step == 0:
        packs, vecs = (None, None), []
    else:
        packs, sums_in, vecs, refs = refs[:2], refs[2], refs[3 : 3 + step], refs[3 + step :]
    total_ref, sums_ref = refs
    blocks = Blocks(step, psi_ref, packs, vecs[-1] if vecs else None, (), last)
    sums = Sums(step + 1, blocks.size)
    for k in range(BLOCKS):
        terms = [term for term in range(4) if blocks.near(k, term)]
        if not terms:
            continue
        total = blocks.energy(k, energy_ref) * blocks.own(k).astype(jnp.float32)
        for term in terms:
            total = total + blocks.term(k, term, left_ref, right_ref)
        total_ref[k] = total
    for k in range(BLOCKS):
        if step == 0:
            vals = psi_ref[k // 2, k % 2].astype(jnp.float32)
            sums.add(0, vals, vals)
            continue
        own = blocks.own(k).astype(jnp.float32)
        sums.add(0, blocks.start(k).astype(jnp.float32), own)
        for place, vec in enumerate(vecs[:-1]):
            sums.add(place + 1, vec[k].astype(jnp.float32), own)
        sums.add(step, own, own)
    row = jnp.zeros((1, 128), jnp.float32) if step == 0 else sums_in[0:1]
    sums_ref[...] = jnp.broadcast_to(sums.write(row, FIRST_SUM[step]), sums_ref.shape)


def far_kernel(step, last, *refs):
    energy_ref, left_ref, right_ref, psi_ref, *refs = refs
    packs, total_ref, refs = refs[:2], refs[2], refs[3:]
    final = step == ITERS - 1
    if final:
        sums_in, vecs, refs = refs[0], refs[1 : 1 + step], refs[1 + step :]
    else:
        vecs, refs = refs[: min(step, 1)], refs[min(step, 1) :]
    halos = 3 if step == 0 else 2
    halo_refs, refs = refs[:halos], refs[halos:]
    blocks = Blocks(step, psi_ref, packs, vecs[-1] if vecs else None, halo_refs, last)
    if final:
        new_ref, back_left, back_right, sums_ref = refs
        sums = Sums(step + 2, blocks.size)
    else:
        new_ref, to_top, to_low = refs
    for k in range(BLOCKS):
        far = [term for term in range(4) if not blocks.near(k, term)]
        if len(far) == 4:
            total = blocks.energy(k, energy_ref) * blocks.own(k).astype(jnp.float32)
        else:
            total = total_ref[k]
        for term in far:
            total = total + blocks.term(k, term, left_ref, right_ref)
        image = total.astype(jnp.bfloat16)
        new_ref[k] = image
        if final:
            vals = image.astype(jnp.float32)
            sums.add(0, blocks.start(k).astype(jnp.float32), vals)
            for place, vec in enumerate(vecs):
                sums.add(place + 1, vec[k].astype(jnp.float32), vals)
            sums.add(step + 1, vals, vals)
            if k not in HELD:
                out, first = (back_right, 0) if k == 1 else (back_left, ITERS * PACKED[k])
                for place, vec in enumerate(vecs):
                    out[first + place] = vec[k]
                out[first + step] = image
        elif k == 0:
            to_low[0] = masked(image, not_at(last))
        elif k == 1:
            to_low[1] = image
        elif k == 6:
            to_top[0] = masked(image, not_at(1))
        elif k == 7:
            to_top[1] = image
    if final:
        row = sums.write(sums_in[0:1], FIRST_SUM[ITERS])
        sums_ref[...] = jnp.broadcast_to(row, sums_ref.shape)


def recursion(gram, coefs):
    def quad(left, right):
        return sum(
            left[i] * right[j] * gram[min(i, j)][max(i, j)]
            for i in range(len(left))
            for j in range(len(right))
        )

    scale = lax.rsqrt(gram[0][0] + eps)
    vec, previous = [scale], []
    thetas, fine = [], jnp.ones_like(scale)
    for step in range(ITERS):
        moved = [jnp.zeros_like(scale)] + vec
        theta = quad(vec, [SHIFT * entry for entry in vec]) + quad(vec, moved)
        thetas.append(theta)
        resid = list(moved)
        for i, entry in enumerate(vec):
            resid[i] = resid[i] + (SHIFT - theta) * entry
        for i, entry in enumerate(previous):
            resid[i] = resid[i] - coefs[step] * entry
        norm_sq = quad(resid, resid)
        lead = resid[-1]
        held = lead * lead * gram[step + 1][step + 1] <= SHRINK * (norm_sq + eps)
        fine = jnp.where(held, fine, 0.0)
        norm = lax.rsqrt(jnp.maximum(norm_sq, 0.0) + eps)
        previous = vec
        vec = [entry * norm for entry in resid]
    return vec, thetas, fine


def combine_kernel(count, num_ref, den_ref, sums_ref, psi_ref, one_ref, two_ref, three_ref, right_back, left_back, out_ref, row_ref):
    sums = jnp.sum(sums_ref[...], axis=0, keepdims=True) * count
    lanes = lax.broadcasted_iota(jnp.int32, sums.shape, 1)
    entries = [
        jnp.sum(jnp.where(lanes == place, sums, 0.0), axis=1, keepdims=True) for place in range(SUMS)
    ]
    gram = [[None] * (ITERS + 1) for _ in range(ITERS + 1)]
    place = 0
    for right in range(ITERS + 1):
        for left in range(right + 1):
            gram[left][right] = entries[place]
            place += 1
    coefs = [jnp.zeros_like(entries[0])]
    for step in range(ITERS - 1):
        num = jnp.full(entries[0].shape, num_ref[step], jnp.int32).astype(jnp.float32)
        den = jnp.full(entries[0].shape, den_ref[step], jnp.int32).astype(jnp.float32)
        coefs.append(num / den)
    weights, thetas, fine = recursion(gram, coefs)
    row = jnp.zeros((1, 128), jnp.float32)
    for place, value in enumerate(thetas + [fine]):
        row = place_in(row, place, value)
    row_ref[...] = row
    held = {where: k for k, where in HELD.items()}
    back = {(0, 0): (left_back, 0), (2, 1): (right_back, 0), (3, 0): (right_back, 1), (3, 1): (right_back, 2)}
    for i in range(ROWS):
        for j in range(COLS):
            blocks = [psi_ref[i, j]]
            if (i, j) in held:
                blocks += [ref[held[i, j]] for ref in (one_ref, two_ref, three_ref)]
            else:
                ref, place = back[i, j]
                blocks += [ref[ITERS * place + step] for step in range(ITERS)]
            total = weights[0] * blocks[0].astype(jnp.float32)
            for weight, block in zip(weights[1:], blocks[1:]):
                total = total + weight * block.astype(jnp.float32)
            out_ref[i, j] = total.astype(jnp.bfloat16)


def move(block, down, right, skipped=None):
    rows, cols = lax.axis_size("lsec"), lax.axis_size("rsec")
    pairs = [
        (row * cols + col, (row + down) * cols + (col + right) % cols)
        for row in range(rows)
        for col in range(cols)
        if 0 <= row + down < rows and col != skipped
    ]
    return lax.ppermute(block, AXES, pairs)


def call(kernel, in_specs, out_shapes, flops, *args):
    nbytes = sum(a.size * a.dtype.itemsize for a in args)
    nbytes += sum(s.size * s.dtype.itemsize for s in out_shapes)
    return pl.pallas_call(
        kernel,
        in_specs=in_specs,
        out_specs=[VMEM] * len(out_shapes),
        out_shape=out_shapes,
        compiler_params=PARAMS,
        cost_estimate=pl.CostEstimate(flops=flops, bytes_accessed=nbytes, transcendentals=0),
    )(*args)


def per_device(psi, left_env, right_env, energies, coef_num, coef_den):
    size = psi.shape[-1]
    devices = lax.axis_size("lsec") * lax.axis_size("rsec")
    last = lax.axis_size("rsec") - 1
    count = 1.0 / float(psi.size * devices)

    def blocks(number):
        return jax.ShapeDtypeStruct((number, size, size), jnp.bfloat16)

    levels = energies.T
    to_right, to_left, top, low, corner = call(
        pack_kernel,
        [VMEM, VMEM, SMEM],
        [
            jax.ShapeDtypeStruct((11 * size + 144, size), jnp.bfloat16),
            jax.ShapeDtypeStruct((5 * size + 48, size), jnp.bfloat16),
            blocks(2), blocks(1), blocks(1),
        ],
        0, psi, right_env, levels,
    )
    packs = [move(to_right, 0, 1), move(to_left, 0, -1)]
    halos = [move(top, 1, -1), move(low, -1, 2, last), move(corner, -1, 1)]
    fixed = [levels, left_env, right_env, psi]
    row = jax.ShapeDtypeStruct((8, 128), jnp.float32)
    vecs, sums = [], []
    for step in range(ITERS):
        final = step == ITERS - 1
        ins = fixed + (packs + sums + vecs if step else [])
        partial, *sums = call(
            lambda *refs, step=step: near_kernel(step, last, *refs),
            [SMEM] + [VMEM] * (len(ins) - 1),
            [jax.ShapeDtypeStruct((BLOCKS, size, size), jnp.float32), row],
            4 * (28 if step else 12) * size**3, *ins,
        )
        ins = fixed + packs + [partial] + (sums + vecs if final else vecs[-1:]) + halos
        if final:
            outs = [blocks(BLOCKS), blocks(3 * ITERS), blocks(ITERS), jax.ShapeDtypeStruct((devices, 128), jnp.float32)]
        else:
            outs = [blocks(BLOCKS), blocks(2), blocks(2)]
        result = call(
            lambda *refs, step=step: far_kernel(step, last, *refs),
            [SMEM] + [VMEM] * (len(ins) - 1), outs, 4 * (4 if step else 20) * size**3, *ins,
        )
        vecs.append(result[0])
        if not final:
            halos = [move(result[1], 1, -2), move(result[2], -1, 2)]
    right_back = move(result[1], 0, -1)
    left_back = move(result[2], 0, 1)
    gathered = lax.all_to_all(result[3].reshape(devices, 1, 128), AXES, 0, 0).reshape(devices, 128)
    vec, row = call(
        lambda *refs: combine_kernel(count, *refs),
        [SMEM, SMEM] + [VMEM] * 7,
        [jax.ShapeDtypeStruct(psi.shape, jnp.bfloat16), jax.ShapeDtypeStruct((1, 128), jnp.float32)],
        0, coef_num, coef_den, gathered, psi, *vecs, right_back, left_back,
    )
    thetas = row[0, :ITERS]
    return lax.cond(
        row[0, ITERS] > 0.5,
        lambda: (vec, thetas),
        lambda: stepwise(psi, left_env, right_env, energies, coef_num, coef_den, count),
    )


def solution(mesh):
    in_specs = (
        P("lsec", "rsec", None, None),
        P("lsec", None, None, None),
        P("rsec", None, None, None),
        P("lsec", "rsec"),
        P(),
        P(),
    )
    out_specs = (P("lsec", "rsec", None, None), P())
    return jax.shard_map(
        per_device, mesh=mesh, in_specs=in_specs, out_specs=out_specs, check_vma=False
    )
```

```python
import jax
import jax.numpy as jnp
from jax import lax
from jax.experimental import pallas as pl
from jax.experimental.pallas import tpu as pltpu
from jax.sharding import PartitionSpec as P

DIAG = 2
HOPS = 1
ITERS = 3
AXES = ("lsec", "rsec")
eps = 1e-06
SHIFT = 1.75
SHRINK = 8.0


def shift_blocks(block, down, right):
    rows, cols = lax.axis_size("lsec"), lax.axis_size("rsec")
    pairs = [
        (row * cols + col, (row + down) * cols + col + right)
        for row in range(rows)
        for col in range(cols)
        if 0 <= row + down < rows and 0 <= col + right < cols
    ]
    return lax.ppermute(block, AXES, pairs)


def add_terms(left_env, right_env, source, first, number, total):
    for term in range(first, first + number):
        inner = jnp.einsum(
            "aij,abjk->abik", left_env[:, term], source, preferred_element_type=jnp.float32
        ).astype(jnp.bfloat16)
        total = total + jnp.einsum(
            "abik,blk->abil", inner, right_env[:, term], preferred_element_type=jnp.float32
        )
    return total


def matvec(vec, left_env, right_env, energies):
    total = energies[:, :, None, None] * vec.astype(jnp.float32)
    total = add_terms(left_env, right_env, vec, 0, DIAG, total)
    from_right = shift_blocks(vec[:-1, :1], 0, -1)
    from_left = shift_blocks(vec[1:, -1:], 0, 1)
    from_up = shift_blocks(vec[-1:, 1:], 1, 0)
    from_down = shift_blocks(vec[:1, :-1], -1, 0)
    up_right = shift_blocks(vec[-1:, :1], 1, -1)
    down_left = shift_blocks(vec[:1, -1:], -1, 1)
    plus_blocks = jnp.concatenate(
        [
            jnp.concatenate([from_up, up_right], axis=1),
            jnp.concatenate([vec[:-1, 1:], from_right], axis=1),
        ],
        axis=0,
    )
    minus_blocks = jnp.concatenate(
        [
            jnp.concatenate([from_left, vec[1:, :-1]], axis=1),
            jnp.concatenate([down_left, from_down], axis=1),
        ],
        axis=0,
    )
    total = add_terms(left_env, right_env, plus_blocks, DIAG, HOPS, total)
    total = add_terms(left_env, right_env, minus_blocks, DIAG + HOPS, HOPS, total)
    return total


def coefficient(coef_num, coef_den, step):
    if step == 0:
        return jnp.float32(0.0)
    return coef_num[step - 1].astype(jnp.float32) / coef_den[step - 1].astype(jnp.float32)


def stepwise(psi, left_env, right_env, energies, coef_num, coef_den, count):
    start_vals = psi.astype(jnp.float32)
    start = lax.psum(jnp.sum(start_vals * start_vals), AXES) * count
    vec = (start_vals * lax.rsqrt(start + eps)).astype(jnp.bfloat16)
    previous = jnp.zeros(psi.shape, jnp.float32)
    thetas = []
    for step in range(ITERS):
        sigma = matvec(vec, left_env, right_env, energies)
        vals = vec.astype(jnp.float32)
        coef = coefficient(coef_num, coef_den, step)
        theta = lax.psum(jnp.sum(vals * sigma), AXES) * count
        resid = sigma - theta * vals - coef * previous
        norm_sq = lax.psum(jnp.sum(resid * resid), AXES) * count
        thetas.append(theta)
        previous = vals
        vec = (resid * lax.rsqrt(norm_sq + eps)).astype(jnp.bfloat16)
    return (vec, jnp.stack(thetas))


ROWS, COLS, BLOCKS = 4, 2, 8
SUMS = 10
SIDE_TERMS = 2
VMEM = pl.BlockSpec(memory_space=pltpu.VMEM)
SMEM = pl.BlockSpec(memory_space=pltpu.SMEM)
PARAMS = pltpu.CompilerParams(vmem_limit_bytes=24 * 1024 * 1024)


def dot(left, right):
    return lax.dot_general(
        left, right, (((1,), (0,)), ((), ())), preferred_element_type=jnp.float32
    )


def dot_t(left, right):
    return lax.dot_general(
        left, right, (((1,), (1,)), ((), ())), preferred_element_type=jnp.float32
    )


def not_at(place):
    return (lax.axis_index("rsec") != place).astype(jnp.float32)


def masked(block, keep):
    return (block.astype(jnp.float32) * keep).astype(jnp.bfloat16)


def write_energy(ref, start, value):
    rest = jnp.full((16, ref.shape[-1]), value, jnp.float32)
    for place in range(3):
        part = rest.astype(jnp.bfloat16)
        ref[start + 16 * place : start + 16 * place + 16] = part
        rest = rest - part.astype(jnp.float32)


def pack_kernel(psi_ref, right_ref, energy_ref, side_out, right_out, left_out, top_out, low_out, corner_out):
    size = psi_ref.shape[-1]
    for place, (i, j) in enumerate(((2, 1), (3, 0), (3, 1))):
        right_out[place * size : (place + 1) * size] = psi_ref[i, j]
        write_energy(right_out, 5 * size + 48 * place, energy_ref[j, i])
    left_out[:size] = psi_ref[0, 0]
    write_energy(left_out, 5 * size, energy_ref[0, 0])
    for term in range(4):
        side_out[term] = right_ref[0, term]
        if term < SIDE_TERMS:
            side_out[4 + term] = right_ref[1, term]
        else:
            start = (3 + term - SIDE_TERMS) * size
            right_out[start : start + size] = right_ref[1, term]
        left_out[(1 + term) * size : (2 + term) * size] = right_ref[0, term]
    top_out[0] = masked(psi_ref[3, 0], not_at(0))
    top_out[1] = psi_ref[3, 1]
    low_out[0] = psi_ref[0, 1]
    corner_out[0] = psi_ref[0, 0]


def place_in(row, lane, value):
    lanes = lax.broadcasted_iota(jnp.int32, row.shape, row.ndim - 1)
    return jnp.where(lanes == lane, value, row)


HELD = {0: (0, 1), 2: (1, 0), 3: (1, 1), 5: (2, 0)}
PACKED = {4: 0, 6: 1, 7: 2}


class Blocks:
    def __init__(self, step, psi_ref, packs, vec_ref, halo_refs, last):
        self.step, self.psi_ref, self.vec_ref, self.halo_refs = step, psi_ref, vec_ref, halo_refs
        self.side, self.from_left, self.from_right = packs
        self.size = psi_ref.shape[-1]
        first, last = not_at(0), not_at(last)
        self.cut = {(4, 2): first, (7, 5): first, (3, 1): last}

    def start(self, k):
        if k in HELD:
            return self.psi_ref[HELD[k]]
        if k == 1:
            return self.from_right[: self.size]
        return self.from_left[PACKED[k] * self.size : (PACKED[k] + 1) * self.size]

    def own(self, k):
        return self.start(k) if self.step == 0 else self.vec_ref[k]

    def place(self, k, term):
        return k if term < DIAG else k - 2 if term == DIAG else k + 2

    def source(self, k, term):
        place = self.place(k, term)
        if 0 <= place < BLOCKS:
            return self.own(place)
        top = place < 0
        if self.step == 0 and not top:
            return self.halo_refs[1 + k % 2][0]
        return self.halo_refs[0 if top else 1][k % 2]

    def near(self, k, term):
        place = self.place(k, term)
        if self.step == 0:
            return k in HELD and place in HELD
        return 0 <= place < BLOCKS

    def right(self, k, term, right_ref):
        if k in HELD:
            return right_ref[HELD[k][1], term]
        if k == 1:
            return self.from_right[(1 + term) * self.size : (2 + term) * self.size]
        if k == 6:
            return self.side[term]
        if term < SIDE_TERMS:
            return self.side[4 + term]
        start = (3 + term - SIDE_TERMS) * self.size
        return self.from_left[start : start + self.size]

    def term(self, k, term, left_ref, right_ref):
        inner = dot(left_ref[k // 2, term], self.source(k, term))
        place = self.place(k, term)
        keep = self.cut.get((max(k, place), min(k, place))) if term >= DIAG else None
        if keep is not None:
            inner = inner * keep
        return dot_t(inner.astype(jnp.bfloat16), self.right(k, term, right_ref))

    def energy(self, k, energy_ref):
        if k in HELD:
            i, j = HELD[k]
            return energy_ref[j, i] - SHIFT
        ref, start = (self.from_right, 5 * self.size) if k == 1 else (self.from_left, 5 * self.size + 48 * PACKED[k])
        parts = [ref[start + 16 * i : start + 16 * i + 16].astype(jnp.float32) for i in range(3)]
        return sum(parts)[:1] - SHIFT


class Sums:
    def __init__(self, number, size):
        self.size = size
        self.totals = [jnp.zeros((8, size), jnp.float32) for _ in range(number)]

    def add(self, place, one, other):
        product = (one * other).reshape(self.size // 8, 8, self.size)
        self.totals[place] = self.totals[place] + jnp.sum(product, axis=0)

    def write(self, row, first):
        for place, total in enumerate(self.totals):
            value = jnp.sum(jnp.sum(total, axis=0, keepdims=True), axis=1, keepdims=True)
            row = place_in(row, first + place, value)
        return row


FIRST_SUM = (0, 1, 3, 6)


def near_kernel(step, last, *refs):
    energy_ref, left_ref, right_ref, psi_ref, *refs = refs
    if step == 0:
        packs, vecs = (None, None, None), []
    else:
        packs, sums_in, vecs, refs = refs[:3], refs[3], refs[4 : 4 + step], refs[4 + step :]
    total_ref, sums_ref = refs
    blocks = Blocks(step, psi_ref, packs, vecs[-1] if vecs else None, (), last)
    sums = Sums(step + 1, blocks.size)
    for k in range(BLOCKS):
        terms = [term for term in range(4) if blocks.near(k, term)]
        if not terms:
            continue
        total = blocks.energy(k, energy_ref) * blocks.own(k).astype(jnp.float32)
        for term in terms:
            total = total + blocks.term(k, term, left_ref, right_ref)
        total_ref[k] = total
    for k in range(BLOCKS):
        if step == 0:
            vals = psi_ref[k // 2, k % 2].astype(jnp.float32)
            sums.add(0, vals, vals)
            continue
        own = blocks.own(k).astype(jnp.float32)
        sums.add(0, blocks.start(k).astype(jnp.float32), own)
        for place, vec in enumerate(vecs[:-1]):
            sums.add(place + 1, vec[k].astype(jnp.float32), own)
        sums.add(step, own, own)
    row = jnp.zeros((1, 128), jnp.float32) if step == 0 else sums_in[0:1]
    sums_ref[...] = jnp.broadcast_to(sums.write(row, FIRST_SUM[step]), sums_ref.shape)


def far_kernel(step, last, *refs):
    energy_ref, left_ref, right_ref, psi_ref, *refs = refs
    packs, total_ref, refs = refs[:3], refs[3], refs[4:]
    final = step == ITERS - 1
    if final:
        sums_in, vecs, refs = refs[0], refs[1 : 1 + step], refs[1 + step :]
    else:
        vecs, refs = refs[: min(step, 1)], refs[min(step, 1) :]
    halos = 3 if step == 0 else 2
    halo_refs, refs = refs[:halos], refs[halos:]
    blocks = Blocks(step, psi_ref, packs, vecs[-1] if vecs else None, halo_refs, last)
    if final:
        new_ref, back_left, back_right, sums_ref = refs
        sums = Sums(step + 2, blocks.size)
    else:
        new_ref, to_top, to_low = refs
    for k in range(BLOCKS):
        far = [term for term in range(4) if not blocks.near(k, term)]
        if len(far) == 4:
            total = blocks.energy(k, energy_ref) * blocks.own(k).astype(jnp.float32)
        else:
            total = total_ref[k]
        for term in far:
            total = total + blocks.term(k, term, left_ref, right_ref)
        image = total.astype(jnp.bfloat16)
        new_ref[k] = image
        if final:
            vals = image.astype(jnp.float32)
            sums.add(0, blocks.start(k).astype(jnp.float32), vals)
            for place, vec in enumerate(vecs):
                sums.add(place + 1, vec[k].astype(jnp.float32), vals)
            sums.add(step + 1, vals, vals)
            if k not in HELD:
                out, first = (back_right, 0) if k == 1 else (back_left, ITERS * PACKED[k])
                for place, vec in enumerate(vecs):
                    out[first + place] = vec[k]
                out[first + step] = image
        elif k == 0:
            to_low[0] = masked(image, not_at(last))
        elif k == 1:
            to_low[1] = image
        elif k == 6:
            to_top[0] = masked(image, not_at(1))
        elif k == 7:
            to_top[1] = image
    if final:
        row = sums.write(sums_in[0:1], FIRST_SUM[ITERS])
        sums_ref[...] = jnp.broadcast_to(row, sums_ref.shape)


def recursion(gram, coefs):
    def quad(left, right):
        return sum(
            left[i] * right[j] * gram[min(i, j)][max(i, j)]
            for i in range(len(left))
            for j in range(len(right))
        )

    scale = lax.rsqrt(gram[0][0] + eps)
    vec, previous = [scale], []
    thetas, fine = [], jnp.ones_like(scale)
    for step in range(ITERS):
        moved = [jnp.zeros_like(scale)] + vec
        theta = quad(vec, [SHIFT * entry for entry in vec]) + quad(vec, moved)
        thetas.append(theta)
        resid = list(moved)
        for i, entry in enumerate(vec):
            resid[i] = resid[i] + (SHIFT - theta) * entry
        for i, entry in enumerate(previous):
            resid[i] = resid[i] - coefs[step] * entry
        norm_sq = quad(resid, resid)
        lead = resid[-1]
        held = lead * lead * gram[step + 1][step + 1] <= SHRINK * (norm_sq + eps)
        fine = jnp.where(held, fine, 0.0)
        norm = lax.rsqrt(jnp.maximum(norm_sq, 0.0) + eps)
        previous = vec
        vec = [entry * norm for entry in resid]
    return vec, thetas, fine


def combine_kernel(count, num_ref, den_ref, sums_ref, psi_ref, one_ref, two_ref, three_ref, right_back, left_back, out_ref, theta_ref, fine_ref):
    sums = jnp.sum(sums_ref[...], axis=0, keepdims=True) * count
    lanes = lax.broadcasted_iota(jnp.int32, sums.shape, 1)
    entries = [
        jnp.sum(jnp.where(lanes == place, sums, 0.0), axis=1, keepdims=True) for place in range(SUMS)
    ]
    gram = [[None] * (ITERS + 1) for _ in range(ITERS + 1)]
    place = 0
    for right in range(ITERS + 1):
        for left in range(right + 1):
            gram[left][right] = entries[place]
            place += 1
    coefs = [jnp.zeros_like(entries[0])]
    for step in range(ITERS - 1):
        num = jnp.full(entries[0].shape, num_ref[step], jnp.int32).astype(jnp.float32)
        den = jnp.full(entries[0].shape, den_ref[step], jnp.int32).astype(jnp.float32)
        coefs.append(num / den)
    weights, thetas, fine = recursion(gram, coefs)
    for place, value in enumerate(thetas):
        theta_ref[place] = jnp.max(value)
    fine_ref[0] = jnp.max(fine)
    held = {where: k for k, where in HELD.items()}
    back = {(0, 0): (left_back, 0), (2, 1): (right_back, 0), (3, 0): (right_back, 1), (3, 1): (right_back, 2)}
    for i in range(ROWS):
        for j in range(COLS):
            blocks = [psi_ref[i, j]]
            if (i, j) in held:
                blocks += [ref[held[i, j]] for ref in (one_ref, two_ref, three_ref)]
            else:
                ref, place = back[i, j]
                blocks += [ref[ITERS * place + step] for step in range(ITERS)]
            total = weights[0] * blocks[0].astype(jnp.float32)
            for weight, block in zip(weights[1:], blocks[1:]):
                total = total + weight * block.astype(jnp.float32)
            out_ref[i, j] = total.astype(jnp.bfloat16)


def move(block, down, right, skipped=None):
    rows, cols = lax.axis_size("lsec"), lax.axis_size("rsec")
    pairs = []
    for row in range(rows):
        target = row ^ 1 if down == "twin" else row + down
        for col in range(cols):
            if 0 <= target < rows and col != skipped:
                pairs.append((row * cols + col, target * cols + (col + right) % cols))
    return lax.ppermute(block, AXES, pairs)


def call(kernel, in_specs, out_shapes, flops, *args):
    nbytes = sum(a.size * a.dtype.itemsize for a in args)
    nbytes += sum(s.size * s.dtype.itemsize for s in out_shapes)
    return pl.pallas_call(
        kernel,
        in_specs=in_specs,
        out_specs=[SMEM if len(shape.shape) == 1 else VMEM for shape in out_shapes],
        out_shape=out_shapes,
        compiler_params=PARAMS,
        cost_estimate=pl.CostEstimate(flops=flops, bytes_accessed=nbytes, transcendentals=0),
    )(*args)


def per_device(psi, left_env, right_env, energies, coef_num, coef_den):
    size = psi.shape[-1]
    devices = lax.axis_size("lsec") * lax.axis_size("rsec")
    last = lax.axis_size("rsec") - 1
    count = 1.0 / float(psi.size * devices)

    def blocks(number):
        return jax.ShapeDtypeStruct((number, size, size), jnp.bfloat16)

    levels = energies.T
    side, to_right, to_left, top, low, corner = call(
        pack_kernel,
        [VMEM, VMEM, SMEM],
        [
            blocks(4 + SIDE_TERMS),
            jax.ShapeDtypeStruct((5 * size + 144, size), jnp.bfloat16),
            jax.ShapeDtypeStruct((5 * size + 48, size), jnp.bfloat16),
            blocks(2), blocks(1), blocks(1),
        ],
        0, psi, right_env, levels,
    )
    packs = [move(side, "twin", 1), move(to_right, 0, 1), move(to_left, 0, -1)]
    halos = [move(top, 1, -1), move(low, -1, 2, last), move(corner, -1, 1)]
    fixed = [levels, left_env, right_env, psi]
    row = jax.ShapeDtypeStruct((8, 128), jnp.float32)
    vecs, sums = [], []
    for step in range(ITERS):
        final = step == ITERS - 1
        ins = fixed + (packs + sums + vecs if step else [])
        partial, *sums = call(
            lambda *refs, step=step: near_kernel(step, last, *refs),
            [SMEM] + [VMEM] * (len(ins) - 1),
            [jax.ShapeDtypeStruct((BLOCKS, size, size), jnp.float32), row],
            4 * (28 if step else 12) * size**3, *ins,
        )
        ins = fixed + packs + [partial] + (sums + vecs if final else vecs[-1:]) + halos
        if final:
            outs = [blocks(BLOCKS), blocks(3 * ITERS), blocks(ITERS), jax.ShapeDtypeStruct((devices, 128), jnp.float32)]
        else:
            outs = [blocks(BLOCKS), blocks(2), blocks(2)]
        result = call(
            lambda *refs, step=step: far_kernel(step, last, *refs),
            [SMEM] + [VMEM] * (len(ins) - 1), outs, 4 * (4 if step else 20) * size**3, *ins,
        )
        vecs.append(result[0])
        if not final:
            halos = [move(result[1], 1, -2), move(result[2], -1, 2)]
    right_back = move(result[1], 0, -1)
    left_back = move(result[2], 0, 1)
    gathered = lax.all_to_all(result[3].reshape(devices, 1, 128), AXES, 0, 0).reshape(devices, 128)
    vec, thetas, fine = call(
        lambda *refs: combine_kernel(count, *refs),
        [SMEM, SMEM] + [VMEM] * 7,
        [
            jax.ShapeDtypeStruct(psi.shape, jnp.bfloat16),
            jax.ShapeDtypeStruct((ITERS,), jnp.float32),
            jax.ShapeDtypeStruct((1,), jnp.float32),
        ],
        0, coef_num, coef_den, gathered, psi, *vecs, right_back, left_back,
    )
    return lax.cond(
        fine[0] > 0.5,
        lambda: (vec, thetas),
        lambda: stepwise(psi, left_env, right_env, energies, coef_num, coef_den, count),
    )


def solution(mesh):
    in_specs = (
        P("lsec", "rsec", None, None),
        P("lsec", None, None, None),
        P("rsec", None, None, None),
        P("lsec", "rsec"),
        P(),
        P(),
    )
    out_specs = (P("lsec", "rsec", None, None), P())
    return jax.shard_map(
        per_device, mesh=mesh, in_specs=in_specs, out_specs=out_specs, check_vma=False
    )
```

```python
import jax
import jax.numpy as jnp
from jax import lax
from jax.experimental import pallas as pl
from jax.experimental.pallas import tpu as pltpu
from jax.sharding import PartitionSpec as P

DIAG = 2
HOPS = 1
ITERS = 3
AXES = ("lsec", "rsec")
eps = 1e-06
SHIFT = 1.75
SHRINK = 8.0


def shift_blocks(block, down, right):
    rows, cols = lax.axis_size("lsec"), lax.axis_size("rsec")
    pairs = [
        (row * cols + col, (row + down) * cols + col + right)
        for row in range(rows)
        for col in range(cols)
        if 0 <= row + down < rows and 0 <= col + right < cols
    ]
    return lax.ppermute(block, AXES, pairs)


def add_terms(left_env, right_env, source, first, number, total):
    for term in range(first, first + number):
        inner = jnp.einsum(
            "aij,abjk->abik", left_env[:, term], source, preferred_element_type=jnp.float32
        ).astype(jnp.bfloat16)
        total = total + jnp.einsum(
            "abik,blk->abil", inner, right_env[:, term], preferred_element_type=jnp.float32
        )
    return total


def matvec(vec, left_env, right_env, energies):
    total = energies[:, :, None, None] * vec.astype(jnp.float32)
    total = add_terms(left_env, right_env, vec, 0, DIAG, total)
    from_right = shift_blocks(vec[:-1, :1], 0, -1)
    from_left = shift_blocks(vec[1:, -1:], 0, 1)
    from_up = shift_blocks(vec[-1:, 1:], 1, 0)
    from_down = shift_blocks(vec[:1, :-1], -1, 0)
    up_right = shift_blocks(vec[-1:, :1], 1, -1)
    down_left = shift_blocks(vec[:1, -1:], -1, 1)
    plus_blocks = jnp.concatenate(
        [
            jnp.concatenate([from_up, up_right], axis=1),
            jnp.concatenate([vec[:-1, 1:], from_right], axis=1),
        ],
        axis=0,
    )
    minus_blocks = jnp.concatenate(
        [
            jnp.concatenate([from_left, vec[1:, :-1]], axis=1),
            jnp.concatenate([down_left, from_down], axis=1),
        ],
        axis=0,
    )
    total = add_terms(left_env, right_env, plus_blocks, DIAG, HOPS, total)
    total = add_terms(left_env, right_env, minus_blocks, DIAG + HOPS, HOPS, total)
    return total


def coefficient(coef_num, coef_den, step):
    if step == 0:
        return jnp.float32(0.0)
    return coef_num[step - 1].astype(jnp.float32) / coef_den[step - 1].astype(jnp.float32)


def stepwise(psi, left_env, right_env, energies, coef_num, coef_den, count):
    start_vals = psi.astype(jnp.float32)
    start = lax.psum(jnp.sum(start_vals * start_vals), AXES) * count
    vec = (start_vals * lax.rsqrt(start + eps)).astype(jnp.bfloat16)
    previous = jnp.zeros(psi.shape, jnp.float32)
    thetas = []
    for step in range(ITERS):
        sigma = matvec(vec, left_env, right_env, energies)
        vals = vec.astype(jnp.float32)
        coef = coefficient(coef_num, coef_den, step)
        theta = lax.psum(jnp.sum(vals * sigma), AXES) * count
        resid = sigma - theta * vals - coef * previous
        norm_sq = lax.psum(jnp.sum(resid * resid), AXES) * count
        thetas.append(theta)
        previous = vals
        vec = (resid * lax.rsqrt(norm_sq + eps)).astype(jnp.bfloat16)
    return (vec, jnp.stack(thetas))


ROWS, COLS, BLOCKS = 4, 2, 8
SUMS = 10
VMEM = pl.BlockSpec(memory_space=pltpu.VMEM)
SMEM = pl.BlockSpec(memory_space=pltpu.SMEM)
PARAMS = pltpu.CompilerParams(vmem_limit_bytes=40 * 1024 * 1024)


def dot(left, right):
    return lax.dot_general(
        left, right, (((1,), (0,)), ((), ())), preferred_element_type=jnp.float32
    )


def dot_t(left, right):
    return lax.dot_general(
        left, right, (((1,), (1,)), ((), ())), preferred_element_type=jnp.float32
    )


def not_at(place):
    return (lax.axis_index("rsec") != place).astype(jnp.float32)


def masked(block, keep):
    return (block.astype(jnp.float32) * keep).astype(jnp.bfloat16)


def pack_kernel(last, psi_ref, right_ref, energy_ref, pack_ref, left_out, up_out, corner_out, low_out):
    size = psi_ref.shape[-1]
    inner = not_at(last)
    for place in range(2):
        pack_ref[place * size : (place + 1) * size] = masked(psi_ref[place + 1, 1], inner)
        left_out[place] = psi_ref[place, 0]
    pack_ref[2 * size : 3 * size] = psi_ref[3, 1]
    for term in range(4):
        pack_ref[(3 + term) * size : (4 + term) * size] = right_ref[1, term]
    rest = jnp.full((16, size), energy_ref[1, 3], jnp.float32)
    for place in range(3):
        part = rest.astype(jnp.bfloat16)
        start = 7 * size + 16 * place
        pack_ref[start : start + 16] = part
        rest = rest - part.astype(jnp.float32)
    up_out[0] = psi_ref[3, 1]
    corner_out[0] = psi_ref[3, 0]
    low_out[0] = psi_ref[0, 0]
    low_out[1] = masked(psi_ref[0, 1], inner)


def place_in(row, lane, value):
    lanes = lax.broadcasted_iota(jnp.int32, row.shape, row.ndim - 1)
    return jnp.where(lanes == lane, value, row)


class Blocks:
    def __init__(self, step, psi_ref, pack_ref, vec_ref, halo_refs):
        self.step, self.psi_ref, self.pack_ref, self.vec_ref = step, psi_ref, pack_ref, vec_ref
        self.size = psi_ref.shape[-1]
        self.halo_refs = halo_refs

    def packed(self, place):
        return self.pack_ref[place * self.size : (place + 1) * self.size]

    def start(self, k):
        if k == 6:
            return self.packed(2)
        return self.psi_ref[k // 2, k % 2] if k < 6 else self.psi_ref[3, 0]

    def own(self, k):
        return self.start(k) if self.step == 0 else self.vec_ref[k]

    def source(self, k, term):
        if term < DIAG:
            return self.own(k)
        if term == DIAG:
            halo = {0: (0, 0), 1: (0, 1), 3: (3, 0), 5: (3, 1)}
            inside = {2: 1, 4: 3, 6: 4, 7: 5}
        else:
            halo = {0: (2, 0), 2: (2, 1), 6: (1, 0), 7: (1, 1)}
            inside = {1: 2, 3: 4, 4: 6, 5: 7}
        if k in inside:
            return self.own(inside[k])
        group, place = halo[k]
        if self.step == 0 and group == 0:
            return self.halo_refs[(0, 4)[place]][0]
        if self.step == 0 and group == 2:
            return self.packed(place)
        return self.halo_refs[group][place]

    def near(self, k, term):
        if self.step == 0 and (k == 6 or (k, term) == (4, DIAG + HOPS)):
            return False
        if term < DIAG:
            return True
        return k in ((2, 4, 6, 7) if term == DIAG else (1, 3, 4, 5))

    def term(self, k, term, left_ref, right_ref, first_keep):
        inner = dot(left_ref[k // 2, term], self.source(k, term))
        if (k, term) in ((6, DIAG), (4, DIAG + HOPS)):
            inner = inner * first_keep
        right = self.packed(3 + term) if k == 6 else right_ref[k % 2 if k < 6 else 0, term]
        return dot_t(inner.astype(jnp.bfloat16), right)

    def energy(self, k, energy_ref):
        if k == 6:
            start = 7 * self.size
            parts = [self.pack_ref[start + 16 * i : start + 16 * i + 16].astype(jnp.float32) for i in range(3)]
            return sum(parts)[:1] - SHIFT
        return (energy_ref[k % 2, k // 2] if k < 6 else energy_ref[0, 3]) - SHIFT


class Sums:
    def __init__(self, number, size):
        self.size = size
        self.totals = [jnp.zeros((8, size), jnp.float32) for _ in range(number)]

    def add(self, place, one, other):
        product = (one * other).reshape(self.size // 8, 8, self.size)
        self.totals[place] = self.totals[place] + jnp.sum(product, axis=0)

    def write(self, row, first):
        for place, total in enumerate(self.totals):
            value = jnp.sum(jnp.sum(total, axis=0, keepdims=True), axis=1, keepdims=True)
            row = place_in(row, first + place, value)
        return row


FIRST_SUM = (0, 1, 3, 6)


def near_kernel(step, *refs):
    energy_ref, left_ref, right_ref, psi_ref, *refs = refs
    if step == 0:
        pack_ref, vecs, refs = None, [], refs
    else:
        pack_ref, *refs = refs
        sums_in, *refs = refs
        vecs, refs = refs[:step], refs[step:]
    total_ref, sums_ref = refs
    blocks = Blocks(step, psi_ref, pack_ref, vecs[-1] if vecs else None, ())
    first_keep = not_at(0)
    sums = Sums(step + 1, blocks.size)
    for k in range(BLOCKS):
        terms = [term for term in range(4) if blocks.near(k, term)]
        if not terms:
            continue
        own = blocks.own(k).astype(jnp.float32)
        total = blocks.energy(k, energy_ref) * own
        for term in terms:
            total = total + blocks.term(k, term, left_ref, right_ref, first_keep)
        total_ref[k] = total
    for k in range(BLOCKS):
        if step == 0:
            vals = psi_ref[k // 2, k % 2].astype(jnp.float32)
            sums.add(0, vals, vals)
            continue
        own = blocks.own(k).astype(jnp.float32)
        sums.add(0, blocks.start(k).astype(jnp.float32), own)
        for place, vec in enumerate(vecs[:-1]):
            sums.add(place + 1, vec[k].astype(jnp.float32), own)
        sums.add(step, own, own)
    row = jnp.zeros((1, 128), jnp.float32) if step == 0 else sums_in[0:1]
    sums_ref[...] = jnp.broadcast_to(sums.write(row, FIRST_SUM[step]), sums_ref.shape)


def far_kernel(step, last, *refs):
    energy_ref, left_ref, right_ref, psi_ref, pack_ref, total_ref, *refs = refs
    final = step == ITERS - 1
    if final:
        sums_in, *refs = refs
        vecs, refs = refs[:step], refs[step:]
    elif step > 0:
        vecs, refs = refs[:1], refs[1:]
    else:
        vecs = []
    halos = 4
    halo_refs, refs = refs[:halos], refs[halos:]
    if step == 0:
        up, low, left, corner = halo_refs
        halo_refs = (up, low, None, left, corner)
    blocks = Blocks(step, psi_ref, pack_ref, vecs[-1] if vecs else None, halo_refs)
    first_keep, last_keep = not_at(0), not_at(last)
    if final:
        new_ref, back_ref, sums_ref = refs
        sums = Sums(step + 2, blocks.size)
    else:
        new_ref, to_top, to_low, to_left, to_right = refs
    for k in (0, 1, 6, 7, 2, 3, 4, 5):
        far = [term for term in range(4) if not blocks.near(k, term)]
        if len(far) == 4:
            total = blocks.energy(k, energy_ref) * blocks.own(k).astype(jnp.float32)
        else:
            total = total_ref[k]
        for term in far:
            total = total + blocks.term(k, term, left_ref, right_ref, first_keep)
        image = total.astype(jnp.bfloat16)
        new_ref[k] = image
        if final:
            vals = image.astype(jnp.float32)
            sums.add(0, blocks.start(k).astype(jnp.float32), vals)
            for place, vec in enumerate(vecs):
                sums.add(place + 1, vec[k].astype(jnp.float32), vals)
            sums.add(step + 1, vals, vals)
            if k == 6:
                for place, vec in enumerate(vecs):
                    back_ref[place] = vec[k]
                back_ref[step] = image
            continue
        for place, out, slot, keep in (
            (0, to_left, 0, None), (2, to_left, 1, None), (3, to_right, 0, None), (5, to_right, 1, None),
            (6, to_top, 0, None), (7, to_top, 1, first_keep), (0, to_low, 0, None), (1, to_low, 1, last_keep),
        ):
            if place == k:
                out[slot] = image if keep is None else masked(image, keep)
    if final:
        row = sums.write(sums_in[0:1], FIRST_SUM[ITERS])
        sums_ref[...] = jnp.broadcast_to(row, sums_ref.shape)


def recursion(gram, coefs):
    def quad(left, right):
        return sum(
            left[i] * right[j] * gram[min(i, j)][max(i, j)]
            for i in range(len(left))
            for j in range(len(right))
        )

    scale = lax.rsqrt(gram[0][0] + eps)
    vec, previous = [scale], []
    thetas, fine = [], jnp.ones_like(scale)
    for step in range(ITERS):
        moved = [jnp.zeros_like(scale)] + vec
        theta = quad(vec, [SHIFT * entry for entry in vec]) + quad(vec, moved)
        thetas.append(theta)
        resid = list(moved)
        for i, entry in enumerate(vec):
            resid[i] = resid[i] + (SHIFT - theta) * entry
        for i, entry in enumerate(previous):
            resid[i] = resid[i] - coefs[step] * entry
        norm_sq = quad(resid, resid)
        lead = resid[-1]
        held = lead * lead * gram[step + 1][step + 1] <= SHRINK * (norm_sq + eps)
        fine = jnp.where(held, fine, 0.0)
        norm = lax.rsqrt(jnp.maximum(norm_sq, 0.0) + eps)
        previous = vec
        vec = [entry * norm for entry in resid]
    return vec, thetas, fine


def combine_kernel(count, num_ref, den_ref, sums_ref, psi_ref, one_ref, two_ref, three_ref, back_ref, out_ref, theta_ref, fine_ref):
    sums = jnp.sum(sums_ref[...], axis=0, keepdims=True) * count
    lanes = lax.broadcasted_iota(jnp.int32, sums.shape, 1)
    entries = [
        jnp.sum(jnp.where(lanes == place, sums, 0.0), axis=1, keepdims=True) for place in range(SUMS)
    ]
    gram = [[None] * (ITERS + 1) for _ in range(ITERS + 1)]
    place = 0
    for right in range(ITERS + 1):
        for left in range(right + 1):
            gram[left][right] = entries[place]
            place += 1
    coefs = [jnp.zeros_like(entries[0])]
    for step in range(ITERS - 1):
        num = jnp.full(entries[0].shape, num_ref[step], jnp.int32).astype(jnp.float32)
        den = jnp.full(entries[0].shape, den_ref[step], jnp.int32).astype(jnp.float32)
        coefs.append(num / den)
    weights, thetas, fine = recursion(gram, coefs)
    for place, value in enumerate(thetas):
        theta_ref[place] = jnp.max(value)
    fine_ref[0] = jnp.max(fine)
    for i in range(ROWS):
        for j in range(COLS):
            k = 2 * i + j + (i == 3)
            blocks = [psi_ref[i, j]]
            if k == 8:
                blocks += [back_ref[0], back_ref[1], back_ref[2]]
            else:
                blocks += [one_ref[k], two_ref[k], three_ref[k]]
            total = weights[0] * blocks[0].astype(jnp.float32)
            for weight, block in zip(weights[1:], blocks[1:]):
                total = total + weight * block.astype(jnp.float32)
            out_ref[i, j] = total.astype(jnp.bfloat16)


def move(block, down, right, around):
    rows, cols = lax.axis_size("lsec"), lax.axis_size("rsec")
    pairs = [
        (row * cols + col, (row + down) * cols + (col + right) % cols)
        for row in range(rows)
        for col in range(cols)
        if 0 <= row + down < rows and (around or 0 <= col + right < cols)
    ]
    return lax.ppermute(block, AXES, pairs)


def call(kernel, in_specs, out_shapes, flops, *args):
    nbytes = sum(a.size * a.dtype.itemsize for a in args)
    nbytes += sum(s.size * s.dtype.itemsize for s in out_shapes)
    return pl.pallas_call(
        kernel,
        in_specs=in_specs,
        out_specs=[SMEM if len(shape.shape) == 1 else VMEM for shape in out_shapes],
        out_shape=out_shapes,
        compiler_params=PARAMS,
        cost_estimate=pl.CostEstimate(flops=flops, bytes_accessed=nbytes, transcendentals=0),
    )(*args)


def per_device(psi, left_env, right_env, energies, coef_num, coef_den):
    size = psi.shape[-1]
    devices = lax.axis_size("lsec") * lax.axis_size("rsec")
    last = lax.axis_size("rsec") - 1
    count = 1.0 / float(psi.size * devices)

    def blocks(number):
        return jax.ShapeDtypeStruct((number, size, size), jnp.bfloat16)

    levels = energies.T
    pack, to_left, to_up, to_corner, to_low = call(
        lambda *refs: pack_kernel(last, *refs),
        [VMEM, VMEM, SMEM],
        [jax.ShapeDtypeStruct((7 * size + 48, size), jnp.bfloat16), blocks(2), blocks(1), blocks(1), blocks(2)],
        0, psi, right_env, levels,
    )
    pack = move(pack, 0, 1, True)
    to_low = move(to_low, -1, 1, True)
    to_up = move(to_up, 1, 0, False)
    to_corner = move(to_corner, 1, -1, False)
    to_left = move(to_left, 0, -1, False)
    halos = [to_up, to_low, to_left, to_corner]
    fixed = [levels, left_env, right_env, psi]
    row = jax.ShapeDtypeStruct((8, 128), jnp.float32)
    vecs, sums = [], []
    for step in range(ITERS):
        final = step == ITERS - 1
        ins = fixed + ([pack] + sums + vecs if step else [])
        partial, *sums = call(
            lambda *refs, step=step: near_kernel(step, *refs),
            [SMEM] + [VMEM] * (len(ins) - 1),
            [jax.ShapeDtypeStruct((BLOCKS, size, size), jnp.float32), row],
            4 * (24 if step else 20) * size**3, *ins,
        )
        ins = fixed + [pack, partial] + (sums + vecs if final else vecs[-1:]) + halos
        if final:
            outs = [blocks(BLOCKS), blocks(ITERS), jax.ShapeDtypeStruct((devices, 128), jnp.float32)]
        else:
            outs = [blocks(BLOCKS)] + [blocks(2)] * 4
        result = call(
            lambda *refs, step=step: far_kernel(step, last, *refs),
            [SMEM] + [VMEM] * (len(ins) - 1), outs, 4 * (8 if step else 12) * size**3, *ins,
        )
        vecs.append(result[0])
        if not final:
            to_top, to_low, to_left, to_right = result[1:5]
            to_top = move(to_top, 1, -1, True)
            to_low = move(to_low, -1, 1, True)
            to_left = move(to_left, 0, -1, False)
            to_right = move(to_right, 0, 1, False)
            halos = [to_top, to_low, to_right, to_left]
    sums = [result[-1]]
    back = move(result[1], 0, -1, True)
    gathered = lax.all_to_all(sums[0].reshape(devices, 1, 128), AXES, 0, 0).reshape(devices, 128)
    vec, thetas, fine = call(
        lambda *refs: combine_kernel(count, *refs),
        [SMEM, SMEM] + [VMEM] * 6,
        [
            jax.ShapeDtypeStruct(psi.shape, jnp.bfloat16),
            jax.ShapeDtypeStruct((ITERS,), jnp.float32),
            jax.ShapeDtypeStruct((1,), jnp.float32),
        ],
        0, coef_num, coef_den, gathered, psi, *vecs, back,
    )
    return lax.cond(
        fine[0] > 0.5,
        lambda: (vec, thetas),
        lambda: stepwise(psi, left_env, right_env, energies, coef_num, coef_den, count),
    )


def solution(mesh):
    in_specs = (
        P("lsec", "rsec", None, None),
        P("lsec", None, None, None),
        P("rsec", None, None, None),
        P("lsec", "rsec"),
        P(),
        P(),
    )
    out_specs = (P("lsec", "rsec", None, None), P())
    return jax.shard_map(
        per_device, mesh=mesh, in_specs=in_specs, out_specs=out_specs, check_vma=False
    )
```

```python
import jax
import jax.numpy as jnp
from jax import lax
from jax.experimental import pallas as pl
from jax.experimental.pallas import tpu as pltpu
from jax.sharding import PartitionSpec as P

DIAG = 2
HOPS = 1
ITERS = 3
AXES = ("lsec", "rsec")
eps = 1e-06
SHIFT = 1.75
SHRINK = 4.0


def shift_blocks(block, down, right):
    rows, cols = lax.axis_size("lsec"), lax.axis_size("rsec")
    pairs = [
        (row * cols + col, (row + down) * cols + col + right)
        for row in range(rows)
        for col in range(cols)
        if 0 <= row + down < rows and 0 <= col + right < cols
    ]
    return lax.ppermute(block, AXES, pairs)


def add_terms(left_env, right_env, source, first, number, total):
    for term in range(first, first + number):
        inner = jnp.einsum(
            "aij,abjk->abik", left_env[:, term], source, preferred_element_type=jnp.float32
        ).astype(jnp.bfloat16)
        total = total + jnp.einsum(
            "abik,blk->abil", inner, right_env[:, term], preferred_element_type=jnp.float32
        )
    return total


def matvec(vec, left_env, right_env, energies):
    total = energies[:, :, None, None] * vec.astype(jnp.float32)
    total = add_terms(left_env, right_env, vec, 0, DIAG, total)
    from_right = shift_blocks(vec[:-1, :1], 0, -1)
    from_left = shift_blocks(vec[1:, -1:], 0, 1)
    from_up = shift_blocks(vec[-1:, 1:], 1, 0)
    from_down = shift_blocks(vec[:1, :-1], -1, 0)
    up_right = shift_blocks(vec[-1:, :1], 1, -1)
    down_left = shift_blocks(vec[:1, -1:], -1, 1)
    plus_blocks = jnp.concatenate(
        [
            jnp.concatenate([from_up, up_right], axis=1),
            jnp.concatenate([vec[:-1, 1:], from_right], axis=1),
        ],
        axis=0,
    )
    minus_blocks = jnp.concatenate(
        [
            jnp.concatenate([from_left, vec[1:, :-1]], axis=1),
            jnp.concatenate([down_left, from_down], axis=1),
        ],
        axis=0,
    )
    total = add_terms(left_env, right_env, plus_blocks, DIAG, HOPS, total)
    total = add_terms(left_env, right_env, minus_blocks, DIAG + HOPS, HOPS, total)
    return total


def coefficient(coef_num, coef_den, step):
    if step == 0:
        return jnp.float32(0.0)
    return coef_num[step - 1].astype(jnp.float32) / coef_den[step - 1].astype(jnp.float32)


def stepwise(psi, left_env, right_env, energies, coef_num, coef_den, count):
    start_vals = psi.astype(jnp.float32)
    start = lax.psum(jnp.sum(start_vals * start_vals), AXES) * count
    vec = (start_vals * lax.rsqrt(start + eps)).astype(jnp.bfloat16)
    previous = jnp.zeros(psi.shape, jnp.float32)
    thetas = []
    for step in range(ITERS):
        sigma = matvec(vec, left_env, right_env, energies)
        vals = vec.astype(jnp.float32)
        coef = coefficient(coef_num, coef_den, step)
        theta = lax.psum(jnp.sum(vals * sigma), AXES) * count
        resid = sigma - theta * vals - coef * previous
        norm_sq = lax.psum(jnp.sum(resid * resid), AXES) * count
        thetas.append(theta)
        previous = vals
        vec = (resid * lax.rsqrt(norm_sq + eps)).astype(jnp.bfloat16)
    return (vec, jnp.stack(thetas))


ROWS, COLS, BLOCKS = 4, 2, 8
SUMS = 10
VMEM = pl.BlockSpec(memory_space=pltpu.VMEM)
SMEM = pl.BlockSpec(memory_space=pltpu.SMEM)
PARAMS = pltpu.CompilerParams(vmem_limit_bytes=40 * 1024 * 1024)


def dot(left, right):
    return lax.dot_general(
        left, right, (((1,), (0,)), ((), ())), preferred_element_type=jnp.float32
    )


def dot_t(left, right):
    return lax.dot_general(
        left, right, (((1,), (1,)), ((), ())), preferred_element_type=jnp.float32
    )


def not_at(place):
    return (lax.axis_index("rsec") != place).astype(jnp.float32)


def on_first_core():
    return (lax.axis_index("rsec") % 2 == 0).astype(jnp.float32)


def mixed(one, other, share):
    return (one.astype(jnp.float32) * share + other.astype(jnp.float32) * (1.0 - share)).astype(jnp.bfloat16)


def masked(block, keep):
    return (block.astype(jnp.float32) * keep).astype(jnp.bfloat16)


def pack_kernel(last, psi_ref, right_ref, energy_ref, pack_ref, left_out, up_out, corner_out, low_out):
    size = psi_ref.shape[-1]
    inner = not_at(last)
    for place in range(2):
        pack_ref[place * size : (place + 1) * size] = masked(psi_ref[place + 1, 1], inner)
        left_out[place] = psi_ref[place, 0]
    pack_ref[2 * size : 3 * size] = psi_ref[3, 1]
    for term in range(4):
        pack_ref[(3 + term) * size : (4 + term) * size] = right_ref[1, term]
    rest = jnp.full((16, size), energy_ref[1, 3], jnp.float32)
    for place in range(3):
        part = rest.astype(jnp.bfloat16)
        start = 7 * size + 16 * place
        pack_ref[start : start + 16] = part
        rest = rest - part.astype(jnp.float32)
    up_out[0] = psi_ref[3, 1]
    corner_out[0] = psi_ref[3, 0]
    low_out[0] = psi_ref[0, 0]
    low_out[1] = masked(psi_ref[0, 1], inner)


def place_in(row, lane, value):
    lanes = lax.broadcasted_iota(jnp.int32, row.shape, row.ndim - 1)
    return jnp.where(lanes == lane, value, row)


class Blocks:
    def __init__(self, step, psi_ref, pack_ref, vec_ref, halo_refs):
        self.step, self.psi_ref, self.pack_ref, self.vec_ref = step, psi_ref, pack_ref, vec_ref
        self.size = psi_ref.shape[-1]
        self.halo_refs = halo_refs

    def packed(self, place):
        return self.pack_ref[place * self.size : (place + 1) * self.size]

    def start(self, k):
        if k == 6:
            return self.packed(2)
        return self.psi_ref[k // 2, k % 2] if k < 6 else self.psi_ref[3, 0]

    def own(self, k):
        return self.start(k) if self.step == 0 else self.vec_ref[k]

    def source(self, k, term):
        if term < DIAG:
            return self.own(k)
        if term == DIAG:
            halo = {0: (0, 0), 1: (0, 1), 3: (3, 0), 5: (3, 1)}
            inside = {2: 1, 4: 3, 6: 4, 7: 5}
        else:
            halo = {0: (2, 0), 2: (2, 1), 6: (1, 0), 7: (1, 1)}
            inside = {1: 2, 3: 4, 4: 6, 5: 7}
        if k in inside:
            return self.own(inside[k])
        group, place = halo[k]
        if self.step == 0 and group == 0:
            return self.halo_refs[(0, 4)[place]][0]
        if self.step == 0 and group == 2:
            return self.packed(place)
        if self.step > 0 and group > 1:
            near, far = (ref[place] for ref in self.halo_refs[2:])
            return mixed(far, near, on_first_core()) if group == 2 else mixed(near, far, on_first_core())
        return self.halo_refs[group][place]

    def near(self, k, term):
        if self.step == 0 and (k == 6 or (k, term) == (4, DIAG + HOPS)):
            return False
        if term < DIAG:
            return True
        return k in ((2, 4, 6, 7) if term == DIAG else (1, 3, 4, 5))

    def term(self, k, term, left_ref, right_ref, first_keep):
        inner = dot(left_ref[k // 2, term], self.source(k, term))
        if (k, term) in ((6, DIAG), (4, DIAG + HOPS)):
            inner = inner * first_keep
        right = self.packed(3 + term) if k == 6 else right_ref[k % 2 if k < 6 else 0, term]
        return dot_t(inner.astype(jnp.bfloat16), right)

    def energy(self, k, energy_ref):
        if k == 6:
            start = 7 * self.size
            parts = [self.pack_ref[start + 16 * i : start + 16 * i + 16].astype(jnp.float32) for i in range(3)]
            return sum(parts)[:1] - SHIFT
        return (energy_ref[k % 2, k // 2] if k < 6 else energy_ref[0, 3]) - SHIFT


class Sums:
    def __init__(self, number, size):
        self.size = size
        self.totals = [jnp.zeros((8, size), jnp.float32) for _ in range(number)]

    def add(self, place, one, other):
        product = (one * other).reshape(self.size // 8, 8, self.size)
        self.totals[place] = self.totals[place] + jnp.sum(product, axis=0)

    def write(self, row, first):
        for place, total in enumerate(self.totals):
            value = jnp.sum(jnp.sum(total, axis=0, keepdims=True), axis=1, keepdims=True)
            row = place_in(row, first + place, value)
        return row


FIRST_SUM = (0, 1, 3, 6)


def near_kernel(step, *refs):
    energy_ref, left_ref, right_ref, psi_ref, *refs = refs
    if step == 0:
        pack_ref, vecs, refs = None, [], refs
    else:
        pack_ref, *refs = refs
        sums_in, *refs = refs
        vecs, refs = refs[:step], refs[step:]
    total_ref, sums_ref = refs
    blocks = Blocks(step, psi_ref, pack_ref, vecs[-1] if vecs else None, ())
    first_keep = not_at(0)
    sums = Sums(step + 1, blocks.size)
    for k in range(BLOCKS):
        terms = [term for term in range(4) if blocks.near(k, term)]
        if not terms:
            continue
        own = blocks.own(k).astype(jnp.float32)
        total = blocks.energy(k, energy_ref) * own
        for term in terms:
            total = total + blocks.term(k, term, left_ref, right_ref, first_keep)
        total_ref[k] = total
    for k in range(BLOCKS):
        if step == 0:
            vals = psi_ref[k // 2, k % 2].astype(jnp.float32)
            sums.add(0, vals, vals)
            continue
        own = blocks.own(k).astype(jnp.float32)
        sums.add(0, blocks.start(k).astype(jnp.float32), own)
        for place, vec in enumerate(vecs[:-1]):
            sums.add(place + 1, vec[k].astype(jnp.float32), own)
        sums.add(step, own, own)
    row = jnp.zeros((1, 128), jnp.float32) if step == 0 else sums_in[0:1]
    sums_ref[...] = jnp.broadcast_to(sums.write(row, FIRST_SUM[step]), sums_ref.shape)


def far_kernel(step, last, *refs):
    energy_ref, left_ref, right_ref, psi_ref, pack_ref, total_ref, *refs = refs
    final = step == ITERS - 1
    if final:
        sums_in, *refs = refs
        vecs, refs = refs[:step], refs[step:]
    elif step > 0:
        vecs, refs = refs[:1], refs[1:]
    else:
        vecs = []
    halos = 4
    halo_refs, refs = refs[:halos], refs[halos:]
    if step == 0:
        up, low, left, corner = halo_refs
        halo_refs = (up, low, None, left, corner)
    blocks = Blocks(step, psi_ref, pack_ref, vecs[-1] if vecs else None, halo_refs)
    first_keep, last_keep = not_at(0), not_at(last)
    if final:
        new_ref, back_ref, sums_ref = refs
        sums = Sums(step + 2, blocks.size)
    else:
        new_ref, to_top, to_low, to_near, to_far = refs
    for k in (0, 1, 6, 7, 2, 3, 4, 5):
        far = [term for term in range(4) if not blocks.near(k, term)]
        if len(far) == 4:
            total = blocks.energy(k, energy_ref) * blocks.own(k).astype(jnp.float32)
        else:
            total = total_ref[k]
        for term in far:
            total = total + blocks.term(k, term, left_ref, right_ref, first_keep)
        image = total.astype(jnp.bfloat16)
        new_ref[k] = image
        if final:
            vals = image.astype(jnp.float32)
            sums.add(0, blocks.start(k).astype(jnp.float32), vals)
            for place, vec in enumerate(vecs):
                sums.add(place + 1, vec[k].astype(jnp.float32), vals)
            sums.add(step + 1, vals, vals)
            if k == 6:
                for place, vec in enumerate(vecs):
                    back_ref[place] = vec[k]
                back_ref[step] = image
            continue
        for place, out, slot, keep in (
            (6, to_top, 0, None), (7, to_top, 1, first_keep), (0, to_low, 0, None), (1, to_low, 1, last_keep),
        ):
            if place == k:
                out[slot] = image if keep is None else masked(image, keep)
    if not final:
        for slot, (left, right) in enumerate(((0, 3), (2, 5))):
            to_near[slot] = mixed(new_ref[right], new_ref[left], on_first_core())
            to_far[slot] = mixed(new_ref[left], new_ref[right], on_first_core())
    if final:
        row = sums.write(sums_in[0:1], FIRST_SUM[ITERS])
        sums_ref[...] = jnp.broadcast_to(row, sums_ref.shape)


def recursion(gram, coefs):
    def quad(left, right):
        return sum(
            left[i] * right[j] * gram[min(i, j)][max(i, j)]
            for i in range(len(left))
            for j in range(len(right))
        )

    scale = lax.rsqrt(gram[0][0] + eps)
    vec, previous = [scale], []
    thetas, fine = [], jnp.ones_like(scale)
    for step in range(ITERS):
        moved = [jnp.zeros_like(scale)] + vec
        theta = quad(vec, [SHIFT * entry for entry in vec]) + quad(vec, moved)
        thetas.append(theta)
        resid = list(moved)
        for i, entry in enumerate(vec):
            resid[i] = resid[i] + (SHIFT - theta) * entry
        for i, entry in enumerate(previous):
            resid[i] = resid[i] - coefs[step] * entry
        norm_sq = quad(resid, resid)
        lead = resid[-1]
        held = lead * lead * gram[step + 1][step + 1] <= SHRINK * (norm_sq + eps)
        fine = jnp.where(held, fine, 0.0)
        norm = lax.rsqrt(jnp.maximum(norm_sq, 0.0) + eps)
        previous = vec
        vec = [entry * norm for entry in resid]
    return vec, thetas, fine


def combine_kernel(count, num_ref, den_ref, sums_ref, psi_ref, one_ref, two_ref, three_ref, back_ref, out_ref, theta_ref, fine_ref):
    sums = jnp.sum(sums_ref[...], axis=0, keepdims=True) * count
    lanes = lax.broadcasted_iota(jnp.int32, sums.shape, 1)
    entries = [
        jnp.sum(jnp.where(lanes == place, sums, 0.0), axis=1, keepdims=True) for place in range(SUMS)
    ]
    gram = [[None] * (ITERS + 1) for _ in range(ITERS + 1)]
    place = 0
    for right in range(ITERS + 1):
        for left in range(right + 1):
            gram[left][right] = entries[place]
            place += 1
    coefs = [jnp.zeros_like(entries[0])]
    for step in range(ITERS - 1):
        num = jnp.full(entries[0].shape, num_ref[step], jnp.int32).astype(jnp.float32)
        den = jnp.full(entries[0].shape, den_ref[step], jnp.int32).astype(jnp.float32)
        coefs.append(num / den)
    weights, thetas, fine = recursion(gram, coefs)
    for place, value in enumerate(thetas):
        theta_ref[place] = jnp.max(value)
    fine_ref[0] = jnp.max(fine)
    for i in range(ROWS):
        for j in range(COLS):
            k = 2 * i + j + (i == 3)
            blocks = [psi_ref[i, j]]
            if k == 8:
                blocks += [back_ref[0], back_ref[1], back_ref[2]]
            else:
                blocks += [one_ref[k], two_ref[k], three_ref[k]]
            total = weights[0] * blocks[0].astype(jnp.float32)
            for weight, block in zip(weights[1:], blocks[1:]):
                total = total + weight * block.astype(jnp.float32)
            out_ref[i, j] = total.astype(jnp.bfloat16)


def move(block, down, right, around):
    rows, cols = lax.axis_size("lsec"), lax.axis_size("rsec")
    pairs = [
        (row * cols + col, (row + down) * cols + (col + right) % cols)
        for row in range(rows)
        for col in range(cols)
        if 0 <= row + down < rows and (around or 0 <= col + right < cols)
    ]
    return lax.ppermute(block, AXES, pairs)


def swap(block, offset):
    rows, cols = lax.axis_size("lsec"), lax.axis_size("rsec")
    pairs = []
    for row in range(rows):
        for col in range(offset, cols - 1, 2):
            first = row * cols + col
            pairs += [(first, first + 1), (first + 1, first)]
    return lax.ppermute(block, AXES, pairs)


def call(kernel, in_specs, out_shapes, flops, *args):
    nbytes = sum(a.size * a.dtype.itemsize for a in args)
    nbytes += sum(s.size * s.dtype.itemsize for s in out_shapes)
    return pl.pallas_call(
        kernel,
        in_specs=in_specs,
        out_specs=[SMEM if len(shape.shape) == 1 else VMEM for shape in out_shapes],
        out_shape=out_shapes,
        compiler_params=PARAMS,
        cost_estimate=pl.CostEstimate(flops=flops, bytes_accessed=nbytes, transcendentals=0),
    )(*args)


def per_device(psi, left_env, right_env, energies, coef_num, coef_den):
    size = psi.shape[-1]
    devices = lax.axis_size("lsec") * lax.axis_size("rsec")
    last = lax.axis_size("rsec") - 1
    count = 1.0 / float(psi.size * devices)

    def blocks(number):
        return jax.ShapeDtypeStruct((number, size, size), jnp.bfloat16)

    levels = energies.T
    pack, to_left, to_up, to_corner, to_low = call(
        lambda *refs: pack_kernel(last, *refs),
        [VMEM, VMEM, SMEM],
        [jax.ShapeDtypeStruct((7 * size + 48, size), jnp.bfloat16), blocks(2), blocks(1), blocks(1), blocks(2)],
        0, psi, right_env, levels,
    )
    pack = move(pack, 0, 1, True)
    to_low = move(to_low, -1, 1, True)
    to_up = move(to_up, 1, 0, False)
    to_corner = move(to_corner, 1, -1, False)
    to_left = move(to_left, 0, -1, False)
    halos = [to_up, to_low, to_left, to_corner]
    fixed = [levels, left_env, right_env, psi]
    row = jax.ShapeDtypeStruct((8, 128), jnp.float32)
    vecs, sums = [], []
    for step in range(ITERS):
        final = step == ITERS - 1
        ins = fixed + ([pack] + sums + vecs if step else [])
        partial, *sums = call(
            lambda *refs, step=step: near_kernel(step, *refs),
            [SMEM] + [VMEM] * (len(ins) - 1),
            [jax.ShapeDtypeStruct((BLOCKS, size, size), jnp.float32), row],
            4 * (24 if step else 20) * size**3, *ins,
        )
        ins = fixed + [pack, partial] + (sums + vecs if final else vecs[-1:]) + halos
        if final:
            outs = [blocks(BLOCKS), blocks(ITERS), jax.ShapeDtypeStruct((devices, 128), jnp.float32)]
        else:
            outs = [blocks(BLOCKS)] + [blocks(2)] * 4
        result = call(
            lambda *refs, step=step: far_kernel(step, last, *refs),
            [SMEM] + [VMEM] * (len(ins) - 1), outs, 4 * (8 if step else 12) * size**3, *ins,
        )
        vecs.append(result[0])
        if not final:
            to_top, to_low, to_near, to_far = result[1:5]
            to_top = move(to_top, 1, -1, True)
            to_low = move(to_low, -1, 1, True)
            halos = [to_top, to_low, swap(to_near, 0), swap(to_far, 1)]
    sums = [result[-1]]
    back = move(result[1], 0, -1, True)
    gathered = lax.all_to_all(sums[0].reshape(devices, 1, 128), AXES, 0, 0).reshape(devices, 128)
    vec, thetas, fine = call(
        lambda *refs: combine_kernel(count, *refs),
        [SMEM, SMEM] + [VMEM] * 6,
        [
            jax.ShapeDtypeStruct(psi.shape, jnp.bfloat16),
            jax.ShapeDtypeStruct((ITERS,), jnp.float32),
            jax.ShapeDtypeStruct((1,), jnp.float32),
        ],
        0, coef_num, coef_den, gathered, psi, *vecs, back,
    )
    return lax.cond(
        fine[0] > 0.5,
        lambda: (vec, thetas),
        lambda: stepwise(psi, left_env, right_env, energies, coef_num, coef_den, count),
    )


def solution(mesh):
    in_specs = (
        P("lsec", "rsec", None, None),
        P("lsec", None, None, None),
        P("rsec", None, None, None),
        P("lsec", "rsec"),
        P(),
        P(),
    )
    out_specs = (P("lsec", "rsec", None, None), P())
    return jax.shard_map(
        per_device, mesh=mesh, in_specs=in_specs, out_specs=out_specs, check_vma=False
    )
```

```python
import jax
import jax.numpy as jnp
from jax import lax
from jax.experimental import pallas as pl
from jax.experimental.pallas import tpu as pltpu
from jax.sharding import PartitionSpec as P

DIAG = 2
HOPS = 1
ITERS = 3
AXES = ("lsec", "rsec")
eps = 1e-06
SHIFT = 1.75
SHRINK = 4.0


def shift_blocks(block, down, right):
    rows, cols = lax.axis_size("lsec"), lax.axis_size("rsec")
    pairs = [
        (row * cols + col, (row + down) * cols + col + right)
        for row in range(rows)
        for col in range(cols)
        if 0 <= row + down < rows and 0 <= col + right < cols
    ]
    return lax.ppermute(block, AXES, pairs)


def add_terms(left_env, right_env, source, first, number, total):
    for term in range(first, first + number):
        inner = jnp.einsum(
            "aij,abjk->abik", left_env[:, term], source, preferred_element_type=jnp.float32
        ).astype(jnp.bfloat16)
        total = total + jnp.einsum(
            "abik,blk->abil", inner, right_env[:, term], preferred_element_type=jnp.float32
        )
    return total


def matvec(vec, left_env, right_env, energies):
    total = energies[:, :, None, None] * vec.astype(jnp.float32)
    total = add_terms(left_env, right_env, vec, 0, DIAG, total)
    from_right = shift_blocks(vec[:-1, :1], 0, -1)
    from_left = shift_blocks(vec[1:, -1:], 0, 1)
    from_up = shift_blocks(vec[-1:, 1:], 1, 0)
    from_down = shift_blocks(vec[:1, :-1], -1, 0)
    up_right = shift_blocks(vec[-1:, :1], 1, -1)
    down_left = shift_blocks(vec[:1, -1:], -1, 1)
    plus_blocks = jnp.concatenate(
        [
            jnp.concatenate([from_up, up_right], axis=1),
            jnp.concatenate([vec[:-1, 1:], from_right], axis=1),
        ],
        axis=0,
    )
    minus_blocks = jnp.concatenate(
        [
            jnp.concatenate([from_left, vec[1:, :-1]], axis=1),
            jnp.concatenate([down_left, from_down], axis=1),
        ],
        axis=0,
    )
    total = add_terms(left_env, right_env, plus_blocks, DIAG, HOPS, total)
    total = add_terms(left_env, right_env, minus_blocks, DIAG + HOPS, HOPS, total)
    return total


def coefficient(coef_num, coef_den, step):
    if step == 0:
        return jnp.float32(0.0)
    return coef_num[step - 1].astype(jnp.float32) / coef_den[step - 1].astype(jnp.float32)


def stepwise(psi, left_env, right_env, energies, coef_num, coef_den, count):
    start_vals = psi.astype(jnp.float32)
    start = lax.psum(jnp.sum(start_vals * start_vals), AXES) * count
    vec = (start_vals * lax.rsqrt(start + eps)).astype(jnp.bfloat16)
    previous = jnp.zeros(psi.shape, jnp.float32)
    thetas = []
    for step in range(ITERS):
        sigma = matvec(vec, left_env, right_env, energies)
        vals = vec.astype(jnp.float32)
        coef = coefficient(coef_num, coef_den, step)
        theta = lax.psum(jnp.sum(vals * sigma), AXES) * count
        resid = sigma - theta * vals - coef * previous
        norm_sq = lax.psum(jnp.sum(resid * resid), AXES) * count
        thetas.append(theta)
        previous = vals
        vec = (resid * lax.rsqrt(norm_sq + eps)).astype(jnp.bfloat16)
    return (vec, jnp.stack(thetas))


ROWS, COLS, BLOCKS = 4, 2, 8
SUMS = 10
VMEM = pl.BlockSpec(memory_space=pltpu.VMEM)
SMEM = pl.BlockSpec(memory_space=pltpu.SMEM)
PARAMS = pltpu.CompilerParams(vmem_limit_bytes=40 * 1024 * 1024)


def dot(left, right):
    return lax.dot_general(
        left, right, (((1,), (0,)), ((), ())), preferred_element_type=jnp.float32
    )


def dot_t(left, right):
    return lax.dot_general(
        left, right, (((1,), (1,)), ((), ())), preferred_element_type=jnp.float32
    )


def not_at(place):
    return (lax.axis_index("rsec") != place).astype(jnp.float32)


def on_first_core():
    return (lax.axis_index("rsec") % 2 == 0).astype(jnp.float32)


def mixed(one, other, share):
    return (one.astype(jnp.float32) * share + other.astype(jnp.float32) * (1.0 - share)).astype(jnp.bfloat16)


def masked(block, keep):
    return (block.astype(jnp.float32) * keep).astype(jnp.bfloat16)


def pack_kernel(last, psi_ref, right_ref, energy_ref, pack_ref, left_out, up_out, corner_out, low_out, sems):
    size = psi_ref.shape[-1]

    def packed(place):
        return pack_ref.at[place * size : (place + 1) * size]

    pairs = [(psi_ref.at[place + 1, 1], packed(place)) for place in range(3)]
    pairs += [(right_ref.at[1, term], packed(3 + term)) for term in range(4)]
    pairs += [(psi_ref.at[place, 0], left_out.at[place]) for place in range(2)]
    pairs += [(psi_ref.at[3, 1], up_out.at[0]), (psi_ref.at[3, 0], corner_out.at[0])]
    pairs += [(psi_ref.at[0, place], low_out.at[place]) for place in range(2)]
    copies = [pltpu.make_async_copy(source, target, sems.at[i]) for i, (source, target) in enumerate(pairs)]
    for copy in copies:
        copy.start()
    rest = jnp.full((16, size), energy_ref[1, 3], jnp.float32)
    for place in range(3):
        part = rest.astype(jnp.bfloat16)
        start = 7 * size + 16 * place
        pack_ref[start : start + 16] = part
        rest = rest - part.astype(jnp.float32)
    for copy in copies:
        copy.wait()

    @pl.when(lax.axis_index("rsec") == last)
    def _():
        pack_ref[: 2 * size] = jnp.zeros((2 * size, size), jnp.bfloat16)
        low_out[1] = jnp.zeros((size, size), jnp.bfloat16)


def place_in(row, lane, value):
    lanes = lax.broadcasted_iota(jnp.int32, row.shape, row.ndim - 1)
    return jnp.where(lanes == lane, value, row)


class Blocks:
    def __init__(self, step, psi_ref, pack_ref, vec_ref, halo_refs):
        self.step, self.psi_ref, self.pack_ref, self.vec_ref = step, psi_ref, pack_ref, vec_ref
        self.size = psi_ref.shape[-1]
        self.halo_refs = halo_refs

    def packed(self, place):
        return self.pack_ref[place * self.size : (place + 1) * self.size]

    def start(self, k):
        if k == 6:
            return self.packed(2)
        return self.psi_ref[k // 2, k % 2] if k < 6 else self.psi_ref[3, 0]

    def own(self, k):
        return self.start(k) if self.step == 0 else self.vec_ref[k]

    def source(self, k, term):
        if term < DIAG:
            return self.own(k)
        if term == DIAG:
            halo = {0: (0, 0), 1: (0, 1), 3: (3, 0), 5: (3, 1)}
            inside = {2: 1, 4: 3, 6: 4, 7: 5}
        else:
            halo = {0: (2, 0), 2: (2, 1), 6: (1, 0), 7: (1, 1)}
            inside = {1: 2, 3: 4, 4: 6, 5: 7}
        if k in inside:
            return self.own(inside[k])
        group, place = halo[k]
        if self.step == 0 and group == 0:
            return self.halo_refs[(0, 4)[place]][0]
        if self.step == 0 and group == 2:
            return self.packed(place)
        if self.step > 0 and group > 1:
            near, far = (ref[place] for ref in self.halo_refs[2:])
            return mixed(far, near, on_first_core()) if group == 2 else mixed(near, far, on_first_core())
        return self.halo_refs[group][place]

    def near(self, k, term):
        if self.step == 0 and (k == 6 or (k, term) == (4, DIAG + HOPS)):
            return False
        if term < DIAG:
            return True
        return k in ((2, 4, 6, 7) if term == DIAG else (1, 3, 4, 5))

    def term(self, k, term, left_ref, right_ref, first_keep):
        inner = dot(left_ref[k // 2, term], self.source(k, term))
        if (k, term) in ((6, DIAG), (4, DIAG + HOPS)):
            inner = inner * first_keep
        right = self.packed(3 + term) if k == 6 else right_ref[k % 2 if k < 6 else 0, term]
        return dot_t(inner.astype(jnp.bfloat16), right)

    def energy(self, k, energy_ref):
        if k == 6:
            start = 7 * self.size
            parts = [self.pack_ref[start + 16 * i : start + 16 * i + 16].astype(jnp.float32) for i in range(3)]
            return sum(parts)[:1] - SHIFT
        return (energy_ref[k % 2, k // 2] if k < 6 else energy_ref[0, 3]) - SHIFT


class Sums:
    def __init__(self, number, size):
        self.size = size
        self.totals = [jnp.zeros((8, size), jnp.float32) for _ in range(number)]

    def add(self, place, one, other):
        product = (one * other).reshape(self.size // 8, 8, self.size)
        self.totals[place] = self.totals[place] + jnp.sum(product, axis=0)

    def write(self, row, first):
        for place, total in enumerate(self.totals):
            value = jnp.sum(jnp.sum(total, axis=0, keepdims=True), axis=1, keepdims=True)
            row = place_in(row, first + place, value)
        return row


FIRST_SUM = (0, 1, 3, 6)


def near_kernel(step, *refs):
    energy_ref, left_ref, right_ref, psi_ref, *refs = refs
    if step == 0:
        pack_ref, vecs, refs = None, [], refs
    else:
        pack_ref, *refs = refs
        sums_in, *refs = refs
        vecs, refs = refs[:step], refs[step:]
    total_ref, sums_ref = refs
    blocks = Blocks(step, psi_ref, pack_ref, vecs[-1] if vecs else None, ())
    first_keep = not_at(0)
    sums = Sums(step + 1, blocks.size)
    for k in range(BLOCKS):
        terms = [term for term in range(4) if blocks.near(k, term)]
        if not terms:
            continue
        own = blocks.own(k).astype(jnp.float32)
        total = blocks.energy(k, energy_ref) * own
        for term in terms:
            total = total + blocks.term(k, term, left_ref, right_ref, first_keep)
        total_ref[k] = total
    for k in range(BLOCKS):
        if step == 0:
            vals = psi_ref[k // 2, k % 2].astype(jnp.float32)
            sums.add(0, vals, vals)
            continue
        own = blocks.own(k).astype(jnp.float32)
        sums.add(0, blocks.start(k).astype(jnp.float32), own)
        for place, vec in enumerate(vecs[:-1]):
            sums.add(place + 1, vec[k].astype(jnp.float32), own)
        sums.add(step, own, own)
    row = jnp.zeros((1, 128), jnp.float32) if step == 0 else sums_in[0:1]
    sums_ref[...] = jnp.broadcast_to(sums.write(row, FIRST_SUM[step]), sums_ref.shape)


def far_kernel(step, last, *refs):
    energy_ref, left_ref, right_ref, psi_ref, pack_ref, total_ref, *refs = refs
    final = step == ITERS - 1
    if final:
        sums_in, *refs = refs
        vecs, refs = refs[:step], refs[step:]
    elif step > 0:
        vecs, refs = refs[:1], refs[1:]
    else:
        vecs = []
    halos = 4
    halo_refs, refs = refs[:halos], refs[halos:]
    if step == 0:
        up, low, left, corner = halo_refs
        halo_refs = (up, low, None, left, corner)
    blocks = Blocks(step, psi_ref, pack_ref, vecs[-1] if vecs else None, halo_refs)
    first_keep, last_keep = not_at(0), not_at(last)
    if final:
        new_ref, back_ref, sums_ref = refs
        sums = Sums(step + 2, blocks.size)
    else:
        new_ref, to_top, to_low, to_near, to_far = refs
    for k in (0, 1, 6, 7, 2, 3, 4, 5):
        far = [term for term in range(4) if not blocks.near(k, term)]
        if len(far) == 4:
            total = blocks.energy(k, energy_ref) * blocks.own(k).astype(jnp.float32)
        else:
            total = total_ref[k]
        for term in far:
            total = total + blocks.term(k, term, left_ref, right_ref, first_keep)
        image = total.astype(jnp.bfloat16)
        new_ref[k] = image
        if final:
            vals = image.astype(jnp.float32)
            sums.add(0, blocks.start(k).astype(jnp.float32), vals)
            for place, vec in enumerate(vecs):
                sums.add(place + 1, vec[k].astype(jnp.float32), vals)
            sums.add(step + 1, vals, vals)
            if k == 6:
                for place, vec in enumerate(vecs):
                    back_ref[place] = vec[k]
                back_ref[step] = image
            continue
        for place, out, slot, keep in (
            (6, to_top, 0, None), (7, to_top, 1, first_keep), (0, to_low, 0, None), (1, to_low, 1, last_keep),
        ):
            if place == k:
                out[slot] = image if keep is None else masked(image, keep)
    if not final:
        for slot, (left, right) in enumerate(((0, 3), (2, 5))):
            to_near[slot] = mixed(new_ref[right], new_ref[left], on_first_core())
            to_far[slot] = mixed(new_ref[left], new_ref[right], on_first_core())
    if final:
        row = sums.write(sums_in[0:1], FIRST_SUM[ITERS])
        sums_ref[...] = jnp.broadcast_to(row, sums_ref.shape)


def recursion(gram, coefs):
    def quad(left, right):
        return sum(
            left[i] * right[j] * gram[min(i, j)][max(i, j)]
            for i in range(len(left))
            for j in range(len(right))
        )

    scale = lax.rsqrt(gram[0][0] + eps)
    vec, previous = [scale], []
    thetas, fine = [], jnp.ones_like(scale)
    for step in range(ITERS):
        moved = [jnp.zeros_like(scale)] + vec
        theta = quad(vec, [SHIFT * entry for entry in vec]) + quad(vec, moved)
        thetas.append(theta)
        resid = list(moved)
        for i, entry in enumerate(vec):
            resid[i] = resid[i] + (SHIFT - theta) * entry
        for i, entry in enumerate(previous):
            resid[i] = resid[i] - coefs[step] * entry
        norm_sq = quad(resid, resid)
        lead = resid[-1]
        held = lead * lead * gram[step + 1][step + 1] <= SHRINK * (norm_sq + eps)
        fine = jnp.where(held, fine, 0.0)
        norm = lax.rsqrt(jnp.maximum(norm_sq, 0.0) + eps)
        previous = vec
        vec = [entry * norm for entry in resid]
    return vec, thetas, fine


def combine_kernel(count, num_ref, den_ref, sums_ref, psi_ref, one_ref, two_ref, three_ref, back_ref, out_ref, theta_ref, fine_ref):
    sums = jnp.sum(sums_ref[...], axis=0, keepdims=True) * count
    lanes = lax.broadcasted_iota(jnp.int32, sums.shape, 1)
    entries = [
        jnp.sum(jnp.where(lanes == place, sums, 0.0), axis=1, keepdims=True) for place in range(SUMS)
    ]
    gram = [[None] * (ITERS + 1) for _ in range(ITERS + 1)]
    place = 0
    for right in range(ITERS + 1):
        for left in range(right + 1):
            gram[left][right] = entries[place]
            place += 1
    coefs = [jnp.zeros_like(entries[0])]
    for step in range(ITERS - 1):
        num = jnp.full(entries[0].shape, num_ref[step], jnp.int32).astype(jnp.float32)
        den = jnp.full(entries[0].shape, den_ref[step], jnp.int32).astype(jnp.float32)
        coefs.append(num / den)
    weights, thetas, fine = recursion(gram, coefs)
    for place, value in enumerate(thetas):
        theta_ref[place] = jnp.max(value)
    fine_ref[0] = jnp.max(fine)
    for i in range(ROWS):
        for j in range(COLS):
            k = 2 * i + j + (i == 3)
            blocks = [psi_ref[i, j]]
            if k == 8:
                blocks += [back_ref[0], back_ref[1], back_ref[2]]
            else:
                blocks += [one_ref[k], two_ref[k], three_ref[k]]
            total = weights[0] * blocks[0].astype(jnp.float32)
            for weight, block in zip(weights[1:], blocks[1:]):
                total = total + weight * block.astype(jnp.float32)
            out_ref[i, j] = total.astype(jnp.bfloat16)


def move(block, down, right, around):
    rows, cols = lax.axis_size("lsec"), lax.axis_size("rsec")
    pairs = [
        (row * cols + col, (row + down) * cols + (col + right) % cols)
        for row in range(rows)
        for col in range(cols)
        if 0 <= row + down < rows and (around or 0 <= col + right < cols)
    ]
    return lax.ppermute(block, AXES, pairs)


def swap(block, offset):
    rows, cols = lax.axis_size("lsec"), lax.axis_size("rsec")
    pairs = []
    for row in range(rows):
        for col in range(offset, cols - 1, 2):
            first = row * cols + col
            pairs += [(first, first + 1), (first + 1, first)]
    return lax.ppermute(block, AXES, pairs)


def call(kernel, in_specs, out_shapes, flops, *args, scratch=()):
    nbytes = sum(a.size * a.dtype.itemsize for a in args)
    nbytes += sum(s.size * s.dtype.itemsize for s in out_shapes)
    return pl.pallas_call(
        kernel,
        in_specs=in_specs,
        out_specs=[SMEM if len(shape.shape) == 1 else VMEM for shape in out_shapes],
        out_shape=out_shapes,
        scratch_shapes=list(scratch),
        compiler_params=PARAMS,
        cost_estimate=pl.CostEstimate(flops=flops, bytes_accessed=nbytes, transcendentals=0),
    )(*args)


def per_device(psi, left_env, right_env, energies, coef_num, coef_den):
    size = psi.shape[-1]
    devices = lax.axis_size("lsec") * lax.axis_size("rsec")
    last = lax.axis_size("rsec") - 1
    count = 1.0 / float(psi.size * devices)

    def blocks(number):
        return jax.ShapeDtypeStruct((number, size, size), jnp.bfloat16)

    levels = energies.T
    pack, to_left, to_up, to_corner, to_low = call(
        lambda *refs: pack_kernel(last, *refs),
        [pl.BlockSpec(memory_space=pl.ANY)] * 2 + [SMEM],
        [jax.ShapeDtypeStruct((7 * size + 48, size), jnp.bfloat16), blocks(2), blocks(1), blocks(1), blocks(2)],
        0, psi, right_env, levels, scratch=[pltpu.SemaphoreType.DMA((13,))],
    )
    pack = move(pack, 0, 1, True)
    to_low = move(to_low, -1, 1, True)
    to_up = move(to_up, 1, 0, False)
    to_corner = move(to_corner, 1, -1, False)
    to_left = move(to_left, 0, -1, False)
    halos = [to_up, to_low, to_left, to_corner]
    fixed = [levels, left_env, right_env, psi]
    row = jax.ShapeDtypeStruct((8, 128), jnp.float32)
    vecs, sums = [], []
    for step in range(ITERS):
        final = step == ITERS - 1
        ins = fixed + ([pack] + sums + vecs if step else [])
        partial, *sums = call(
            lambda *refs, step=step: near_kernel(step, *refs),
            [SMEM] + [VMEM] * (len(ins) - 1),
            [jax.ShapeDtypeStruct((BLOCKS, size, size), jnp.float32), row],
            4 * (24 if step else 20) * size**3, *ins,
        )
        ins = fixed + [pack, partial] + (sums + vecs if final else vecs[-1:]) + halos
        if final:
            outs = [blocks(BLOCKS), blocks(ITERS), jax.ShapeDtypeStruct((devices, 128), jnp.float32)]
        else:
            outs = [blocks(BLOCKS)] + [blocks(2)] * 4
        result = call(
            lambda *refs, step=step: far_kernel(step, last, *refs),
            [SMEM] + [VMEM] * (len(ins) - 1), outs, 4 * (8 if step else 12) * size**3, *ins,
        )
        vecs.append(result[0])
        if not final:
            to_top, to_low, to_near, to_far = result[1:5]
            to_top = move(to_top, 1, -1, True)
            to_low = move(to_low, -1, 1, True)
            halos = [to_top, to_low, swap(to_near, 0), swap(to_far, 1)]
    sums = [result[-1]]
    back = move(result[1], 0, -1, True)
    gathered = lax.all_to_all(sums[0].reshape(devices, 1, 128), AXES, 0, 0).reshape(devices, 128)
    vec, thetas, fine = call(
        lambda *refs: combine_kernel(count, *refs),
        [SMEM, SMEM] + [VMEM] * 6,
        [
            jax.ShapeDtypeStruct(psi.shape, jnp.bfloat16),
            jax.ShapeDtypeStruct((ITERS,), jnp.float32),
            jax.ShapeDtypeStruct((1,), jnp.float32),
        ],
        0, coef_num, coef_den, gathered, psi, *vecs, back,
    )
    return lax.cond(
        fine[0] > 0.5,
        lambda: (vec, thetas),
        lambda: stepwise(psi, left_env, right_env, energies, coef_num, coef_den, count),
    )


def solution(mesh):
    in_specs = (
        P("lsec", "rsec", None, None),
        P("lsec", None, None, None),
        P("rsec", None, None, None),
        P("lsec", "rsec"),
        P(),
        P(),
    )
    out_specs = (P("lsec", "rsec", None, None), P())
    return jax.shard_map(
        per_device, mesh=mesh, in_specs=in_specs, out_specs=out_specs, check_vma=False
    )
```
